256 devices in a mesh: section: 4 (over x_hi, core), dp: 64 (over z, y, x_lo).
Axes of the slice: x: 4 (x_hi: 2, x_lo: 2; x = x_hi * 2 + x_lo), y: 4, z: 8, core: 2. Of those that a mesh axis runs over, the one named last changes fastest.
Arguments:
- top_grad: bfloat16 [16384, 3584], P('dp'), may hold values from -6 to 6
- activations: bfloat16 [4, 16384, 3584], P('section', 'dp'), may hold values from -6 to 6
- weights: bfloat16 [4, 3584, 3584], P('section', 'dp'), may hold values from -0.09375 to 0.09375
- proj_in: bfloat16 [4, 64, 3584], P('section'), may hold values from -0.09375 to 0.09375
- proj_out: bfloat16 [4, 64, 3584], P('section'), may hold values from -0.09375 to 0.09375
- queries: bfloat16 [4, 128, 4096], P('section', 'dp'), may hold values from -6 to 6
- lengths: int32 [128], P('dp'), may hold values from 32 to 128
Outputs:
- scores: float32 [128, 128], P('dp', 'section')
The draws below stay inside these ranges and needn't reach their ends.
All inputs are finite; a program needn't handle non-finite values.
Results may differ from the reference program's by a relative error of at most 0.013.
Values may be sent and summed in bfloat16 or wider, within the bound.
A program may use at most 128 MiB of HBM per device.

```python
import jax
import jax.numpy as jnp

D = 3584
R = 64
SEQ = 128
SEQS = 128
TOKENS = 16384
QUERIES = 128
N_SECTION = 4


def plant(values, stream_key, least, top_value):
    index_at = [jax.random.randint(jax.random.fold_in(stream_key, axis), (), 0, length) for axis, length in enumerate(values.shape)]
    longest = values.shape.index(max(values.shape))
    beside = index_at[:longest] + [(index_at[longest] + 1) % values.shape[longest]] + index_at[longest + 1:]
    return values.at[tuple(index_at)].set(least).at[tuple(beside)].set(top_value)


def steps_of(stream_key, dims, cuts, smallest, high):
    def one(dim, shards_of):
        draws = jax.random.uniform(jax.random.fold_in(jax.random.fold_in(stream_key, 6), dim), (shards_of,), jnp.float32, smallest / len(cuts), high / len(cuts))
        return jnp.repeat(jnp.exp(draws), dims[dim] // shards_of).reshape((-1,) + (1,) * (len(dims) - dim - 1))

    gain = one(*cuts[0])
    for cut in cuts[1:]:
        gain = gain * one(*cut)
    return gain


def centred(stream_key, dims, width, bound, pieces=(), kind=jnp.bfloat16):
    level = steps_of(stream_key, dims, pieces, -0.22, 0.18) if pieces else 1.0
    drawn = jax.random.normal(stream_key, dims, jnp.float32) * width * level
    return jnp.minimum(jnp.maximum(drawn, -bound), bound).astype(kind)


def setup_inputs(seed: int = 0) -> dict:
    keys = jax.random.split(jax.random.key(seed), 8)
    return {
        "top_grad": centred(keys[0], (TOKENS, D), 1.0, 6.0, ((0, 64),)),
        "activations": centred(keys[1], (N_SECTION, TOKENS, D), 1.0, 6.0, ((0, 4), (1, 64))),
        "weights": centred(keys[2], (N_SECTION, D, D), D ** -0.5, 0.09375, ((0, 4), (1, 64))),
        "proj_in": centred(keys[3], (N_SECTION, R, D), D ** -0.5, 0.09375, ((0, 4),)),
        "proj_out": centred(keys[4], (N_SECTION, R, D), D ** -0.5, 0.09375, ((0, 4),)),
        "queries": centred(keys[5], (N_SECTION, QUERIES, R * R), 1.0, 6.0, ((0, 4), (1, 64))),
        "lengths": plant(jax.random.randint(keys[6], (SEQS,), SEQ // 4, SEQ + 1), jax.random.fold_in(keys[6], 1), SEQ // 4, SEQ).astype(jnp.int32),
    }


def reference(top_grad, activations, weights, proj_in, proj_out, queries, lengths):
    positions = jnp.arange(SEQ, dtype=jnp.int32)
    live_mask = (positions[None, :] < lengths[:, None]).astype(jnp.float32).reshape(SEQS * SEQ, 1)
    cotangent = (top_grad.astype(jnp.float32) * live_mask).astype(jnp.bfloat16)
    length_f = lengths.astype(jnp.float32)
    scores = jnp.zeros((SEQS, QUERIES), jnp.float32)
    for layer in range(N_SECTION - 1, -1, -1):
        x_proj = jnp.dot(activations[layer], proj_in[layer].T, preferred_element_type=jnp.float32).astype(jnp.bfloat16)
        g_proj = jnp.dot(cotangent, proj_out[layer].T, preferred_element_type=jnp.float32).astype(jnp.bfloat16)
        g_seq = g_proj.reshape(SEQS, SEQ, R).astype(jnp.float32)
        x_seq = x_proj.reshape(SEQS, SEQ, R).astype(jnp.float32)
        sketch = jnp.einsum("nta,ntb->nab", g_seq, x_seq) / length_f[:, None, None]
        sketch = sketch.astype(jnp.bfloat16).reshape(SEQS, R * R)
        scores = scores + jnp.dot(sketch, queries[layer].T, preferred_element_type=jnp.float32)
        backward = jnp.dot(cotangent, weights[layer].T, preferred_element_type=jnp.float32)
        cotangent = (cotangent.astype(jnp.float32) + backward).astype(jnp.bfloat16)
    return scores * 0.125
```

```python
import functools

import jax
import jax.numpy as jnp
from jax import lax
from jax.experimental import pallas as pl
from jax.experimental.pallas import tpu as pltpu
from jax.sharding import PartitionSpec as P

D = 3584
R = 64
ROWS = 56
SEQ = 128
TOK = 256
MESH = pl.DeviceIdType.MESH
F32 = jnp.float32
BF16 = jnp.bfloat16
OFFSETS = (4, 3, 5, 2, 6, 1, 7, 0)
PLANE = tuple((a, b) for a in (2, 1, 3, 0) for b in (1, 0) if a or b)


def nt(a, b):
    return lax.dot_general(a, b, (((1,), (1,)), ((), ())), preferred_element_type=F32)


def kernel(
    top_ref, act_ref, w_ref, pin_ref, pout_ref, qry_ref, len_ref, out_ref,
    w_v, win_v, qry_v, pin_v, pout_v, act_v, top_v,
    wt, le, rr, s0_s, s0_r, ob, pb, zs, zb, ag, qb, qf, qg, acc, x2, skf, flat, ex_s, ex_r,
    ld, s0_ss, s0_rs, p_ss, p_rs, z_ss, z_rs, az_ss, az_rs, ap_ss, ap_rs, qz_ss, qz_rs, qp_ss, qp_rs, ex_ss, ex_rs,
):
    s = lax.axis_index("section")
    d = lax.axis_index("dp")
    z = lax.div(d, 8)
    p = lax.rem(d, 8)
    y = lax.div(p, 2)
    x = lax.rem(p, 2)
    lane = lax.broadcasted_iota(jnp.int32, (32, 128), 1)
    low = lane < 64

    def plane(a, b):
        return 2 * lax.rem(y + a, 4) + lax.rem(x + b, 2)

    def remote(src, dst, ss, rs, section, at_z, at_p):
        return pltpu.make_async_remote_copy(
            src_ref=src, dst_ref=dst, send_sem=ss, recv_sem=rs,
            device_id=(section, at_z * 8 + at_p), device_id_type=MESH,
        )

    def wait_bytes(ref, sem):
        pltpu.make_async_copy(ref, ref, sem).wait()

    bar = pltpu.get_barrier_semaphore()
    for dz in OFFSETS:
        for ds in (2, 3, 1, 0):
            if dz or ds:
                pl.semaphore_signal(
                    bar, inc=1, device_id=(lax.rem(s + ds, 4), lax.rem(z + dz, 8) * 8 + p), device_id_type=MESH
                )
    for a, b in PLANE:
        pl.semaphore_signal(bar, inc=1, device_id=(s, z * 8 + plane(a, b)), device_id_type=MESH)

    tile = jnp.minimum(lax.div(ROWS * d, 128), D // 128 - 2)
    loads = [
        pltpu.make_async_copy(pout_ref.at[0, :, pl.ds(pl.multiple_of(tile * 128, 128), 256)], win_v, ld.at[0]),
        pltpu.make_async_copy(w_ref.at[0], w_v, ld.at[1]),
        pltpu.make_async_copy(qry_ref.at[0], qry_v, ld.at[2]),
        pltpu.make_async_copy(act_ref.at[0], act_v, ld.at[3]),
        pltpu.make_async_copy(pin_ref.at[0], pin_v.at[pl.ds(0, R)], ld.at[4]),
        pltpu.make_async_copy(pin_ref.at[0], pin_v.at[pl.ds(R, R)], ld.at[5]),
        pltpu.make_async_copy(top_ref, top_v, ld.at[6]),
        pltpu.make_async_copy(pout_ref.at[0], pout_v.at[pl.ds(0, R)], ld.at[7]),
        pltpu.make_async_copy(pout_ref.at[0], pout_v.at[pl.ds(R, R)], ld.at[8]),
    ]
    for c in loads:
        c.start()

    loads[0].wait()
    first = ROWS * d - 128 * tile
    row = lax.broadcasted_iota(jnp.int32, (32, 256), 0)
    col = lax.broadcasted_iota(jnp.int32, (32, 256), 1) - first
    pick_low = jnp.where(col == row, 1.0, 0.0).astype(BF16)
    pick_high = jnp.where((col == row + 32) & (row < ROWS - 32), 1.0, 0.0).astype(BF16)
    window = win_v[...]
    both = jnp.concatenate([window, window], axis=0)
    s0_s[...] = jnp.where(low, nt(pick_low, both), nt(pick_high, both)).astype(BF16)

    loads[1].wait()

    @pl.when(s >= 1)
    def _():
        @pl.loop(0, D // 128)
        def _(c):
            part = w_v[:, pl.ds(pl.multiple_of(c * 128, 128), 128)].astype(F32)
            gap = jnp.zeros((R - ROWS, 128), F32)
            wt[pl.ds(pl.multiple_of(c * 128, 128), 128), :] = jnp.concatenate([part, gap, part, gap], axis=0).T

        wt[pl.ds(D, 16), :] = jnp.zeros((16, 128), F32)

        @pl.when(s < 3)
        def _():
            @pl.loop(0, 64)
            def _(c):
                one = wt[pl.ds(pl.multiple_of(c * ROWS, 8), 32), :]
                two = wt[pl.ds(pl.multiple_of(c * ROWS + 32, 8), 32), :]
                le[pl.ds(pl.multiple_of(c * 32, 32), 32), pl.ds(0, 128)] = jnp.where(low, one, two).astype(BF16)

        @pl.when(s == 3)
        def _():
            @pl.loop(0, 56)
            def _(c):
                at = lax.div(c, 4) * 256 + lax.rem(c, 4) * 32
                one = wt[pl.ds(pl.multiple_of(at, 32), 32), :]
                two = wt[pl.ds(pl.multiple_of(at + 128, 32), 32), :]
                le[pl.ds(pl.multiple_of(c * 32, 32), 32), pl.ds(0, 128)] = jnp.where(low, one, two).astype(BF16)

            le[pl.ds(1792, 256), pl.ds(0, 128)] = jnp.zeros((256, 128), BF16)

        lane_i = jnp.bitwise_and(lane, 63)
        half = jnp.right_shift(lane, 6)
        sub = lax.broadcasted_iota(jnp.int32, (32, 128), 0)

        @pl.loop(0, 64)
        def _(c):
            inner = ROWS * c + sub + 32 * half
            last = lax.div(c, 4) * 256 + lax.rem(c, 4) * 32 + sub + 128 * half
            at = jnp.where(s == 3, last, inner) - ROWS * d
            hit = (at == lane_i) & (lane_i < ROWS)
            le[pl.ds(pl.multiple_of(c * 32, 32), 32), pl.ds(128, 128)] = jnp.where(hit, 1.0, 0.0).astype(BF16)

    loads[2].wait()
    q32 = qry_v[...].astype(F32)
    for t in range(32):
        qf[pl.ds(t, 1), :] = q32[0:1, 128 * t:128 * t + 128]
        qf[pl.ds(32 + t, 1), :] = q32[1:2, 128 * t:128 * t + 128]
    qb[d] = qf[pl.ds(0, 64), :].astype(BF16)

    pl.semaphore_wait(bar, 38)

    @pl.when(s < 3)
    def _():
        remote(s0_s, s0_r, s0_ss, s0_rs, s + 1, z, p).start()

    def place(packed):
        turned = pltpu.roll(packed, 64, 1)
        zero = jnp.zeros((32, 128), F32)
        parts = (
            jnp.where(low, packed, zero), jnp.where(low, turned, zero),
            jnp.where(low, zero, turned), jnp.where(low, zero, packed),
        )
        for i, part in enumerate(parts):
            rr[pl.ds(32 * i, 32), :] = part.astype(BF16)
            rr[pl.ds(128 + 32 * i, 32), :] = part.astype(BF16)

    def summed(slot):
        wait_bytes(zb.at[slot], z_rs.at[slot])
        total = zb[slot, 0].astype(F32)
        for i in range(1, 8):
            total = total + zb[slot, i].astype(F32)
        return total

    def nth(i):
        return jnp.where(lax.rem(i, 2) == 1, 4 - lax.div(i + 1, 2), 4 + lax.div(i, 2))

    def spread(k):
        @pl.loop(0, 8)
        def _(i):
            to_z = lax.rem(z + nth(i), 8)
            at = pl.ds(pl.multiple_of(to_z * 256, 256), 256)
            ob[k, to_z] = jnp.dot(le[at, :], rr[...], preferred_element_type=F32).astype(BF16).reshape(8, 32, 128)
            for j, (a, b) in enumerate(PLANE):
                to_p = plane(a, b)
                remote(ob.at[k, to_z, to_p], pb.at[k, to_z, j], p_ss.at[k], p_rs.at[k, to_z], s, z, to_p).start()

    def relay(k):
        to_s = jnp.where(s == 3, 2 - k, s + 1)
        slot = jnp.where(s == 3, 1, k)

        @pl.loop(0, 8)
        def _(i):
            to_z = lax.rem(z + nth(i), 8)
            wait_bytes(pb.at[k, to_z], p_rs.at[k, to_z])
            total = ob[k, to_z, p].astype(F32)
            for j in range(7):
                total = total + pb[k, to_z, j].astype(F32)
            zs[k, to_z] = total.astype(BF16)
            remote(zs.at[k, to_z], zb.at[slot, z], z_ss.at[k], z_rs.at[slot], to_s, to_z, p).start()

    def projected(tokens, both_proj):
        acc[...] = jnp.zeros((TOK, 128), F32)

        @pl.loop(0, 7)
        def _(c):
            at = pl.ds(pl.multiple_of(c * 512, 512), 512)
            acc[...] += nt(tokens[:, at], both_proj[:, at])

    @pl.when(s >= 1)
    def _():
        wait_bytes(s0_r, s0_rs)
        place(s0_r[...].astype(F32))
        spread(0)

    for dz in OFFSETS[:-1]:
        to_z = lax.rem(z + dz, 8)
        remote(qb.at[d], qb.at[d], qz_ss, qz_rs, s, to_z, p).start()

    for c in loads[3:6]:
        c.wait()
    projected(act_v, pin_v)
    x2[...] = acc[...].astype(BF16)

    @pl.when(s >= 1)
    def _():
        relay(0)

    wait_bytes(qb.at[pl.ds(0, 7)], qz_rs)
    for a, b in PLANE:
        to_p = plane(a, b)

        @pl.loop(0, 8)
        def _(i):
            block = qb.at[i * 8 + p]
            remote(block, block, qp_ss, qp_rs, s, z, to_p).start()

    @pl.when(s >= 2)
    def _():
        place(summed(0))
        spread(1)
        relay(1)

    @pl.when(s == 3)
    def _():
        place(summed(1))
        spread(2)
        relay(2)

    wait_bytes(qb.at[pl.ds(0, 56)], qp_rs)

    @pl.loop(0, 64)
    def _(c):
        qf[pl.ds(pl.multiple_of(c * 64, 64), 64), :] = qb[c].astype(F32)

    for t in range(32):
        qg[:, 128 * t:128 * t + 128] = qf[pl.ds(t, 128, stride=32), :].astype(BF16)

    for c in loads[6:9]:
        c.wait()

    @pl.when(s == 3)
    def _():
        projected(top_v, pout_v)

    @pl.when(s < 3)
    def _():
        ag[d] = summed(1).astype(BF16)
        for dz in OFFSETS[:-1]:
            remote(ag.at[d], ag.at[d], az_ss, az_rs.at[z], s, lax.rem(z + dz, 8), p).start()

        for dz in (0, 1, 7, 2, 6, 3, 5, 4):
            from_z = lax.rem(z + dz, 8)
            block = ag.at[from_z * 8 + p]
            if dz:
                wait_bytes(block, az_rs.at[from_z])
            for a, b in PLANE:
                remote(block, block, ap_ss, ap_rs.at[from_z], s, z, plane(a, b)).start()
        acc[...] = jnp.zeros((TOK, 128), F32)
        wide = lax.broadcasted_iota(jnp.int32, (128, 128), 1) < 64
        for dz in (0, 1, 7, 2, 6, 3, 5, 4):
            from_z = lax.rem(z + dz, 8)
            wait_bytes(ag.at[pl.ds(0, 7)], ap_rs.at[from_z])

            @pl.when(from_z < 7)
            def _():
                for c in range(2):
                    piece = ag[pl.ds(from_z * 8 + 4 * c, 4)].reshape(128, 128)
                    zero = jnp.zeros_like(piece)
                    rhs = jnp.concatenate([jnp.where(wide, piece, zero), jnp.where(wide, zero, piece)], axis=0)
                    at = pl.ds(pl.multiple_of(from_z * 512 + 256 * c, 256), 256)
                    acc[...] += jnp.dot(top_v[:, at], rhs, preferred_element_type=F32)
        acc[...] = acc[...] + pltpu.roll(acc[...], 64, 1)

    position = lax.broadcasted_iota(jnp.int32, (SEQ, 128), 0)
    flat[...] = jnp.zeros((16, R * R), F32)
    for n in range(2):
        length = len_ref[n]
        rows = pl.ds(n * SEQ, SEQ)
        g = jnp.where(position < length, acc[rows, :], 0.0).astype(BF16)
        skf[...] = lax.dot_general(g, x2[rows, :], (((0,), (0,)), ((), ())), preferred_element_type=F32)
        pairs = jnp.where(low, skf[pl.ds(0, 32, stride=2), :], skf[pl.ds(1, 32, stride=2), :])
        pairs = pairs / jnp.full((32, 128), length, jnp.int32).astype(F32)
        for t in range(32):
            flat[pl.ds(n, 1), 128 * t:128 * t + 128] = pairs[t:t + 1, :]
    part = nt(flat[...].astype(BF16), qg[...])[0:8]
    ex_s[...] = part
    for j in range(1, 4):
        remote(ex_s, ex_r.at[j - 1], ex_ss, ex_rs, lax.rem(s + j, 4), z, p).start()
    wait_bytes(ex_r, ex_rs)
    total = ((part + ex_r[0]) + (ex_r[1] + ex_r[2])) * 0.125
    mine = jnp.zeros((8, 32), F32)
    for i in range(4):
        mine = mine + jnp.where(s == i, total[:, 32 * i:32 * i + 32], 0.0)
    out_ref[...] = mine[0:2, :]

    wait_bytes(ex_r, ex_ss)
    wait_bytes(qb.at[pl.ds(0, 7)], qz_ss)
    wait_bytes(qb.at[pl.ds(0, 56)], qp_ss)

    @pl.when(s < 3)
    def _():
        wait_bytes(s0_s, s0_ss)
        wait_bytes(ag.at[pl.ds(0, 7)], az_ss)
        wait_bytes(ag.at[pl.ds(0, 56)], ap_ss)

    for k in range(3):
        @pl.when(s >= k + 1)
        def _():
            wait_bytes(pb.at[k], p_ss.at[k])
            wait_bytes(zs.at[k], z_ss.at[k])


def local(top_grad, activations, weights, proj_in, proj_out, queries, lengths):
    dma = pltpu.SemaphoreType.DMA
    anywhere = pl.BlockSpec(memory_space=pl.ANY)
    return pl.pallas_call(
        kernel,
        out_shape=jax.ShapeDtypeStruct((2, 32), F32),
        in_specs=[anywhere] * 6 + [pl.BlockSpec(memory_space=pltpu.SMEM)],
        out_specs=pl.BlockSpec(memory_space=pltpu.VMEM),
        scratch_shapes=[
            pltpu.VMEM((ROWS, D), BF16),
            pltpu.VMEM((R, 256), BF16),
            pltpu.VMEM((2, R * R), BF16),
            pltpu.VMEM((2 * R, D), BF16),
            pltpu.VMEM((2 * R, D), BF16),
            pltpu.VMEM((TOK, D), BF16),
            pltpu.VMEM((TOK, D), BF16),
            pltpu.VMEM((D + 16, 128), F32),
            pltpu.VMEM((2048, 256), BF16),
            pltpu.VMEM((256, 128), BF16),
            pltpu.VMEM((32, 128), BF16),
            pltpu.VMEM((32, 128), BF16),
            pltpu.VMEM((3, 8, 8, 32, 128), BF16),
            pltpu.VMEM((3, 8, 7, 32, 128), BF16),
            pltpu.VMEM((3, 8, 32, 128), BF16),
            pltpu.VMEM((2, 8, 32, 128), BF16),
            pltpu.VMEM((64, 32, 128), BF16),
            pltpu.VMEM((64, 64, 128), BF16),
            pltpu.VMEM((4096, 128), F32),
            pltpu.VMEM((128, R * R), BF16),
            pltpu.VMEM((TOK, 128), F32),
            pltpu.VMEM((TOK, 128), BF16),
            pltpu.VMEM((128, 128), F32),
            pltpu.VMEM((16, R * R), F32),
            pltpu.VMEM((8, 128), F32),
            pltpu.VMEM((3, 8, 128), F32),
            dma((9,)),
            dma, dma,
            dma((3,)), dma((3, 8)),
            dma((3,)), dma((2,)),
            dma, dma((8,)),
            dma, dma((8,)),
            dma, dma, dma, dma,
            dma, dma,
        ],
        compiler_params=pltpu.CompilerParams(
            collective_id=0, has_side_effects=True, vmem_limit_bytes=48 * 2**20
        ),
        name="chain",
    )(top_grad, activations, weights, proj_in, proj_out, queries, lengths)


def solution(mesh):
    in_specs = (
        P("dp", None),
        P("section", "dp", None),
        P("section", "dp", None),
        P("section", None, None),
        P("section", None, None),
        P("section", "dp", None),
        P("dp"),
    )
    return jax.shard_map(local, mesh=mesh, in_specs=in_specs, out_specs=P("dp", "section"), check_vma=False)
```

```python
import functools

import jax
import jax.numpy as jnp
from jax import lax
from jax.experimental import pallas as pl
from jax.experimental.pallas import tpu as pltpu
from jax.sharding import PartitionSpec as P

D = 3584
R = 64
ROWS = 56
SEQ = 128
TOK = 256
MESH = pl.DeviceIdType.MESH
F32 = jnp.float32
BF16 = jnp.bfloat16
OFFSETS = (4, 3, 5, 2, 6, 1, 7, 0)
PLANE = tuple((a, b) for a in (2, 1, 3, 0) for b in (1, 0) if a or b)


def nt(a, b):
    return lax.dot_general(a, b, (((1,), (1,)), ((), ())), preferred_element_type=F32)


def kernel(
    top_ref, act_ref, w_ref, pin_ref, pout_ref, qry_ref, len_ref, out_ref,
    w_v, win_v, qry_v, pin_v, pout_v, act_v, top_v,
    wt, le, rr, s0_s, s0_r, ob, pb, zs, zb, ag, qb, qf, qg, acc, x2, skf, flat, ex_s, ex_r,
    ld, s0_ss, s0_rs, p_ss, p_rs, z_ss, z_rs, az_ss, az_rs, ap_ss, ap_rs, qz_ss, qz_rs, qp_ss, qp_rs, ex_ss, ex_rs, gate,
):
    s = lax.axis_index("section")
    d = lax.axis_index("dp")
    z = lax.div(d, 8)
    p = lax.rem(d, 8)
    y = lax.div(p, 2)
    x = lax.rem(p, 2)
    lane = lax.broadcasted_iota(jnp.int32, (32, 128), 1)
    low = lane < 64

    def plane(a, b):
        return 2 * lax.rem(y + a, 4) + lax.rem(x + b, 2)

    def remote(src, dst, ss, rs, section, at_z, at_p):
        return pltpu.make_async_remote_copy(
            src_ref=src, dst_ref=dst, send_sem=ss, recv_sem=rs,
            device_id=(section, at_z * 8 + at_p), device_id_type=MESH,
        )

    def wait_bytes(ref, sem):
        pltpu.make_async_copy(ref, ref, sem).wait()

    bar = pltpu.get_barrier_semaphore()
    for dz in OFFSETS[:-1]:
        pl.semaphore_signal(bar, inc=1, device_id=(s, lax.rem(z + dz, 8) * 8 + p), device_id_type=MESH)
    for ds in (2, 3, 1):
        pl.semaphore_signal(bar, inc=1, device_id=(lax.rem(s + ds, 4), d), device_id_type=MESH)
    for a, b in PLANE:
        pl.semaphore_signal(bar, inc=1, device_id=(s, z * 8 + plane(a, b)), device_id_type=MESH)

    tile = jnp.minimum(lax.div(ROWS * d, 128), D // 128 - 2)
    loads = [
        pltpu.make_async_copy(pout_ref.at[0, :, pl.ds(pl.multiple_of(tile * 128, 128), 256)], win_v, ld.at[0]),
        pltpu.make_async_copy(w_ref.at[0], w_v, ld.at[1]),
        pltpu.make_async_copy(qry_ref.at[0], qry_v, ld.at[2]),
        pltpu.make_async_copy(act_ref.at[0], act_v, ld.at[3]),
        pltpu.make_async_copy(pin_ref.at[0], pin_v.at[pl.ds(0, R)], ld.at[4]),
        pltpu.make_async_copy(pin_ref.at[0], pin_v.at[pl.ds(R, R)], ld.at[5]),
        pltpu.make_async_copy(top_ref, top_v, ld.at[6]),
        pltpu.make_async_copy(pout_ref.at[0], pout_v.at[pl.ds(0, R)], ld.at[7]),
        pltpu.make_async_copy(pout_ref.at[0], pout_v.at[pl.ds(R, R)], ld.at[8]),
    ]
    for c in loads:
        c.start()

    @pl.when(s >= 1)
    def _():
        lane_i = jnp.bitwise_and(lane, 63)
        half = jnp.right_shift(lane, 6)
        sub = lax.broadcasted_iota(jnp.int32, (32, 128), 0)

        @pl.loop(0, 64)
        def _(c):
            inner = ROWS * c + sub + 32 * half
            last = lax.div(c, 4) * 256 + lax.rem(c, 4) * 32 + sub + 128 * half
            at = jnp.where(s == 3, last, inner) - ROWS * d
            hit = (at == lane_i) & (lane_i < ROWS)
            le[pl.ds(pl.multiple_of(c * 32, 32), 32), pl.ds(128, 128)] = jnp.where(hit, 1.0, 0.0).astype(BF16)

    loads[0].wait()
    first = ROWS * d - 128 * tile
    row = lax.broadcasted_iota(jnp.int32, (32, 256), 0)
    col = lax.broadcasted_iota(jnp.int32, (32, 256), 1) - first
    pick_low = jnp.where(col == row, 1.0, 0.0).astype(BF16)
    pick_high = jnp.where((col == row + 32) & (row < ROWS - 32), 1.0, 0.0).astype(BF16)
    window = win_v[...]
    both = jnp.concatenate([window, window], axis=0)
    s0_s[...] = jnp.where(low, nt(pick_low, both), nt(pick_high, both)).astype(BF16)

    loads[1].wait()

    @pl.when(s >= 1)
    def _():
        @pl.loop(0, D // 128)
        def _(c):
            part = w_v[:, pl.ds(pl.multiple_of(c * 128, 128), 128)].astype(F32)
            gap = jnp.zeros((R - ROWS, 128), F32)
            wt[pl.ds(pl.multiple_of(c * 128, 128), 128), :] = jnp.concatenate([part, gap, part, gap], axis=0).T

        wt[pl.ds(D, 16), :] = jnp.zeros((16, 128), F32)

        @pl.when(s < 3)
        def _():
            @pl.loop(0, 64)
            def _(c):
                one = wt[pl.ds(pl.multiple_of(c * ROWS, 8), 32), :]
                two = wt[pl.ds(pl.multiple_of(c * ROWS + 32, 8), 32), :]
                le[pl.ds(pl.multiple_of(c * 32, 32), 32), pl.ds(0, 128)] = jnp.where(low, one, two).astype(BF16)

        @pl.when(s == 3)
        def _():
            @pl.loop(0, 56)
            def _(c):
                at = lax.div(c, 4) * 256 + lax.rem(c, 4) * 32
                one = wt[pl.ds(pl.multiple_of(at, 32), 32), :]
                two = wt[pl.ds(pl.multiple_of(at + 128, 32), 32), :]
                le[pl.ds(pl.multiple_of(c * 32, 32), 32), pl.ds(0, 128)] = jnp.where(low, one, two).astype(BF16)

            le[pl.ds(1792, 256), pl.ds(0, 128)] = jnp.zeros((256, 128), BF16)

    loads[2].wait()
    q32 = qry_v[...].astype(F32)
    for t in range(32):
        qf[pl.ds(t, 1), :] = q32[0:1, 128 * t:128 * t + 128]
        qf[pl.ds(32 + t, 1), :] = q32[1:2, 128 * t:128 * t + 128]
    qb[d] = qf[pl.ds(0, 64), :].astype(BF16)

    pl.semaphore_wait(bar, 17)

    @pl.when(s < 3)
    def _():
        remote(s0_s, s0_r, s0_ss, s0_rs, s + 1, z, p).start()

    for dz in OFFSETS[:-1]:
        remote(qb.at[d], qb.at[d], qz_ss, qz_rs, s, lax.rem(z + dz, 8), p).start()

    def place(packed):
        turned = pltpu.roll(packed, 64, 1)
        zero = jnp.zeros((32, 128), F32)
        parts = (
            jnp.where(low, packed, zero), jnp.where(low, turned, zero),
            jnp.where(low, zero, turned), jnp.where(low, zero, packed),
        )
        for i, part in enumerate(parts):
            rr[pl.ds(32 * i, 32), :] = part.astype(BF16)
            rr[pl.ds(128 + 32 * i, 32), :] = part.astype(BF16)

    def summed(slot):
        wait_bytes(zb.at[slot], z_rs.at[slot])
        total = zb[slot, 0].astype(F32)
        for i in range(1, 8):
            total = total + zb[slot, i].astype(F32)
        return total

    def nth(i):
        return jnp.where(lax.rem(i, 2) == 1, 4 - lax.div(i + 1, 2), 4 + lax.div(i, 2))

    def spread(k):
        @pl.loop(0, 8)
        def _(i):
            to_z = lax.rem(z + nth(i), 8)
            at = pl.ds(pl.multiple_of(to_z * 256, 256), 256)
            ob[k, to_z] = jnp.dot(le[at, :], rr[...], preferred_element_type=F32).astype(BF16).reshape(8, 32, 128)
            for j, (a, b) in enumerate(PLANE):
                to_p = plane(a, b)
                remote(ob.at[k, to_z, to_p], pb.at[k, to_z, j], p_ss.at[k], p_rs.at[k, to_z], s, z, to_p).start()

    def relay(k):
        to_s = jnp.where(s == 3, 2 - k, s + 1)
        slot = jnp.where(s == 3, 1, k)

        @pl.loop(0, 8)
        def _(i):
            to_z = lax.rem(z + nth(i), 8)
            wait_bytes(pb.at[k, to_z], p_rs.at[k, to_z])
            total = ob[k, to_z, p].astype(F32)
            for j in range(7):
                total = total + pb[k, to_z, j].astype(F32)
            zs[k, to_z] = total.astype(BF16)
            remote(zs.at[k, to_z], zb.at[slot, z], z_ss.at[k], z_rs.at[slot], to_s, to_z, p).start()

    def projected(tokens, both_proj):
        acc[...] = jnp.zeros((TOK, 128), F32)

        @pl.loop(0, 7)
        def _(c):
            at = pl.ds(pl.multiple_of(c * 512, 512), 512)
            acc[...] += nt(tokens[:, at], both_proj[:, at])

    def pass_queries(first):
        for a, b in PLANE:
            to_p = plane(a, b)

            @pl.loop(first, first + 4)
            def _(i):
                block = qb.at[i * 8 + p]
                remote(block, block, qp_ss, qp_rs, s, z, to_p).start()

    def turn_queries():
        wait_bytes(qb.at[pl.ds(0, 56)], qp_rs)

        @pl.loop(0, 64)
        def _(c):
            qf[pl.ds(pl.multiple_of(c * 64, 64), 64), :] = qb[c].astype(F32)

        for t in range(32):
            qg[:, 128 * t:128 * t + 128] = qf[pl.ds(t, 128, stride=32), :].astype(BF16)

    def go_ahead(to_s):
        pl.semaphore_signal(gate, inc=1, device_id=(to_s, d), device_id_type=MESH)

    @pl.when(s >= 1)
    def _():
        wait_bytes(s0_r, s0_rs)
        place(s0_r[...].astype(F32))
        spread(0)

    @pl.when(s == 1)
    def _():
        go_ahead(0)

    wait_bytes(qb.at[pl.ds(0, 7)], qz_rs)

    @pl.when(s >= 1)
    def _():
        relay(0)

    @pl.when(s == 0)
    def _():
        pl.semaphore_wait(gate, 1)

    @pl.when(s != 2)
    def _():
        pass_queries(0)

    @pl.when(s < 2)
    def _():
        pass_queries(4)

    for c in loads[3:6]:
        c.wait()
    projected(act_v, pin_v)
    x2[...] = acc[...].astype(BF16)

    @pl.when(s >= 2)
    def _():
        place(summed(0))

        @pl.when(s == 3)
        def _():
            pl.semaphore_wait(gate, 1)

        spread(1)

        @pl.when(s == 2)
        def _():
            go_ahead(3)

        relay(1)

    @pl.when(s == 2)
    def _():
        pass_queries(0)
        pl.semaphore_wait(gate, 1)

    @pl.when(s == 3)
    def _():
        place(summed(1))
        spread(2)
        go_ahead(2)
        relay(2)

    @pl.when(s >= 2)
    def _():
        pass_queries(4)

    for c in loads[6:9]:
        c.wait()

    @pl.when(s == 3)
    def _():
        projected(top_v, pout_v)

    @pl.when(s < 2)
    def _():
        turn_queries()

    @pl.when(s < 3)
    def _():
        ag[d] = summed(1).astype(BF16)
        for dz in OFFSETS[:-1]:
            remote(ag.at[d], ag.at[d], az_ss, az_rs.at[z], s, lax.rem(z + dz, 8), p).start()
        acc[...] = jnp.zeros((TOK, 128), F32)
        wide = lax.broadcasted_iota(jnp.int32, (128, 128), 1) < 64

        def forward(dz):
            from_z = lax.rem(z + dz, 8)
            block = ag.at[from_z * 8 + p]
            if dz:
                wait_bytes(block, az_rs.at[from_z])
            for a, b in PLANE:
                remote(block, block, ap_ss, ap_rs.at[from_z], s, z, plane(a, b)).start()

        def add(dz):
            from_z = lax.rem(z + dz, 8)
            wait_bytes(ag.at[pl.ds(0, 7)], ap_rs.at[from_z])

            @pl.when(from_z < 7)
            def _():
                parts = []
                for c in range(2):
                    piece = ag[pl.ds(from_z * 8 + 4 * c, 4)].reshape(128, 128)
                    zero = jnp.zeros_like(piece)
                    parts += [jnp.where(wide, piece, zero), jnp.where(wide, zero, piece)]
                at = pl.ds(pl.multiple_of(from_z * 512, 512), 512)
                acc[...] += jnp.dot(top_v[:, at], jnp.concatenate(parts, axis=0), preferred_element_type=F32)

        for step, dz in ((forward, 0), (forward, 1), (forward, 7), (forward, 2), (forward, 6), (add, 0), (forward, 3), (forward, 5),
                         (add, 1), (forward, 4), (add, 7), (add, 2), (add, 6), (add, 3), (add, 5), (add, 4)):
            step(dz)
        acc[...] = acc[...] + pltpu.roll(acc[...], 64, 1)

    @pl.when(s >= 2)
    def _():
        turn_queries()

    position = lax.broadcasted_iota(jnp.int32, (SEQ, 128), 0)
    flat[...] = jnp.zeros((16, R * R), F32)
    for n in range(2):
        length = len_ref[n]
        rows = pl.ds(n * SEQ, SEQ)
        g = jnp.where(position < length, acc[rows, :], 0.0).astype(BF16)
        skf[...] = lax.dot_general(g, x2[rows, :], (((0,), (0,)), ((), ())), preferred_element_type=F32)
        pairs = jnp.where(low, skf[pl.ds(0, 32, stride=2), :], skf[pl.ds(1, 32, stride=2), :])
        pairs = pairs / jnp.full((32, 128), length, jnp.int32).astype(F32)
        for t in range(32):
            flat[pl.ds(n, 1), 128 * t:128 * t + 128] = pairs[t:t + 1, :]
    part = nt(flat[...].astype(BF16), qg[...])[0:8]
    ex_s[...] = part
    for j in range(1, 4):
        remote(ex_s, ex_r.at[j - 1], ex_ss, ex_rs, lax.rem(s + j, 4), z, p).start()
    wait_bytes(ex_r, ex_rs)
    total = ((part + ex_r[0]) + (ex_r[1] + ex_r[2])) * 0.125
    mine = jnp.zeros((8, 32), F32)
    for i in range(4):
        mine = mine + jnp.where(s == i, total[:, 32 * i:32 * i + 32], 0.0)
    out_ref[...] = mine[0:2, :]

    wait_bytes(ex_r, ex_ss)
    wait_bytes(qb.at[pl.ds(0, 7)], qz_ss)
    wait_bytes(qb.at[pl.ds(0, 56)], qp_ss)

    @pl.when(s < 3)
    def _():
        wait_bytes(s0_s, s0_ss)
        wait_bytes(ag.at[pl.ds(0, 7)], az_ss)
        wait_bytes(ag.at[pl.ds(0, 56)], ap_ss)

    for k in range(3):
        @pl.when(s >= k + 1)
        def _():
            wait_bytes(pb.at[k], p_ss.at[k])
            wait_bytes(zs.at[k], z_ss.at[k])


def local(top_grad, activations, weights, proj_in, proj_out, queries, lengths):
    dma = pltpu.SemaphoreType.DMA
    anywhere = pl.BlockSpec(memory_space=pl.ANY)
    return pl.pallas_call(
        kernel,
        out_shape=jax.ShapeDtypeStruct((2, 32), F32),
        in_specs=[anywhere] * 6 + [pl.BlockSpec(memory_space=pltpu.SMEM)],
        out_specs=pl.BlockSpec(memory_space=pltpu.VMEM),
        scratch_shapes=[
            pltpu.VMEM((ROWS, D), BF16),
            pltpu.VMEM((R, 256), BF16),
            pltpu.VMEM((2, R * R), BF16),
            pltpu.VMEM((2 * R, D), BF16),
            pltpu.VMEM((2 * R, D), BF16),
            pltpu.VMEM((TOK, D), BF16),
            pltpu.VMEM((TOK, D), BF16),
            pltpu.VMEM((D + 16, 128), F32),
            pltpu.VMEM((2048, 256), BF16),
            pltpu.VMEM((256, 128), BF16),
            pltpu.VMEM((32, 128), BF16),
            pltpu.VMEM((32, 128), BF16),
            pltpu.VMEM((3, 8, 8, 32, 128), BF16),
            pltpu.VMEM((3, 8, 7, 32, 128), BF16),
            pltpu.VMEM((3, 8, 32, 128), BF16),
            pltpu.VMEM((2, 8, 32, 128), BF16),
            pltpu.VMEM((64, 32, 128), BF16),
            pltpu.VMEM((64, 64, 128), BF16),
            pltpu.VMEM((4096, 128), F32),
            pltpu.VMEM((128, R * R), BF16),
            pltpu.VMEM((TOK, 128), F32),
            pltpu.VMEM((TOK, 128), BF16),
            pltpu.VMEM((128, 128), F32),
            pltpu.VMEM((16, R * R), F32),
            pltpu.VMEM((8, 128), F32),
            pltpu.VMEM((3, 8, 128), F32),
            dma((9,)),
            dma, dma,
            dma((3,)), dma((3, 8)),
            dma((3,)), dma((2,)),
            dma, dma((8,)),
            dma, dma((8,)),
            dma, dma, dma, dma,
            dma, dma,
            pltpu.SemaphoreType.REGULAR,
        ],
        compiler_params=pltpu.CompilerParams(
            collective_id=0, has_side_effects=True, vmem_limit_bytes=64 * 2**20 - 2**17
        ),
        name="chain",
    )(top_grad, activations, weights, proj_in, proj_out, queries, lengths)


def solution(mesh):
    in_specs = (
        P("dp", None),
        P("section", "dp", None),
        P("section", "dp", None),
        P("section", None, None),
        P("section", None, None),
        P("section", "dp", None),
        P("dp"),
    )
    return jax.shard_map(local, mesh=mesh, in_specs=in_specs, out_specs=P("dp", "section"), check_vma=False)
```

```python
import functools

import jax
import jax.numpy as jnp
from jax import lax
from jax.experimental import pallas as pl
from jax.experimental.pallas import tpu as pltpu
from jax.sharding import PartitionSpec as P

D = 3584
R = 64
ROWS = 56
SEQ = 128
TOK = 256
MESH = pl.DeviceIdType.MESH
F32 = jnp.float32
BF16 = jnp.bfloat16
OFFSETS = (4, 3, 5, 2, 6, 1, 7, 0)
PARTS = ((0, 1), (1, 3), (3, 5), (5, 8))
PLANE = tuple((a, b) for a in (2, 1, 3, 0) for b in (1, 0) if a or b)


def nt(a, b):
    return lax.dot_general(a, b, (((1,), (1,)), ((), ())), preferred_element_type=F32)


def kernel(
    top_ref, act_ref, w_ref, pin_ref, pout_ref, qry_ref, len_ref, out_ref,
    w_v, win_v, qry_v, pin_v, pout_v, act_v, top_v,
    wt, le, rr, s0_s, s0_r, ob, pb, zs, zb, ag, qb, q3, qf, qg, qg3, acc, x2, skf, sk_s, sk_r, flat, ex,
    ld, s0_ss, s0_rs, p_ss, p_rs, z_ss, z_rs, az_ss, az_rs, ap_ss, ap_rs, qz_ss, qz_rs, qp_ss, qp_rs,
    q3z_ss, q3z_rs, q3p_ss, q3p_rs, sk_ss, sk_rs, ex_ss, ex_rs, gate, line,
):
    s = lax.axis_index("section")
    d = lax.axis_index("dp")
    z = lax.div(d, 8)
    p = lax.rem(d, 8)
    y = lax.div(p, 2)
    x = lax.rem(p, 2)
    lane = lax.broadcasted_iota(jnp.int32, (32, 128), 1)
    low = lane < 64

    def plane(a, b):
        return 2 * lax.rem(y + a, 4) + lax.rem(x + b, 2)

    def remote(src, dst, ss, rs, section, at_z, at_p):
        return pltpu.make_async_remote_copy(
            src_ref=src, dst_ref=dst, send_sem=ss, recv_sem=rs,
            device_id=(section, at_z * 8 + at_p), device_id_type=MESH,
        )

    def wait_bytes(ref, sem):
        pltpu.make_async_copy(ref, ref, sem).wait()

    bar = pltpu.get_barrier_semaphore()
    for dz in OFFSETS[:-1]:
        pl.semaphore_signal(bar, inc=1, device_id=(s, lax.rem(z + dz, 8) * 8 + p), device_id_type=MESH)
    for ds in (2, 3, 1):
        pl.semaphore_signal(bar, inc=1, device_id=(lax.rem(s + ds, 4), d), device_id_type=MESH)
    for a, b in PLANE:
        pl.semaphore_signal(bar, inc=1, device_id=(s, z * 8 + plane(a, b)), device_id_type=MESH)

    tile = jnp.minimum(lax.div(ROWS * d, 128), D // 128 - 2)
    loads = [
        pltpu.make_async_copy(pout_ref.at[0, :, pl.ds(pl.multiple_of(tile * 128, 128), 256)], win_v, ld.at[0]),
        pltpu.make_async_copy(w_ref.at[0], w_v, ld.at[1]),
        pltpu.make_async_copy(qry_ref.at[0], qry_v, ld.at[2]),
        pltpu.make_async_copy(act_ref.at[0], act_v, ld.at[3]),
        pltpu.make_async_copy(pin_ref.at[0], pin_v.at[pl.ds(0, R)], ld.at[4]),
        pltpu.make_async_copy(pin_ref.at[0], pin_v.at[pl.ds(R, R)], ld.at[5]),
        pltpu.make_async_copy(top_ref, top_v, ld.at[6]),
        pltpu.make_async_copy(pout_ref.at[0], pout_v.at[pl.ds(0, R)], ld.at[7]),
        pltpu.make_async_copy(pout_ref.at[0], pout_v.at[pl.ds(R, R)], ld.at[8]),
    ]
    for c in loads:
        c.start()

    ag[pl.ds(56, 8)] = jnp.zeros((8, 32, 128), BF16)

    @pl.when(s >= 1)
    def _():
        lane_i = jnp.bitwise_and(lane, 63)
        half = jnp.right_shift(lane, 6)
        sub = lax.broadcasted_iota(jnp.int32, (32, 128), 0)
        le[:, pl.ds(128, 128)] = jnp.zeros((2048, 128), BF16)

        def ones(c, at):
            hit = (at - ROWS * d == lane_i) & (lane_i < ROWS)
            le[pl.ds(pl.multiple_of(c * 32, 32), 32), pl.ds(128, 128)] = jnp.where(hit, 1.0, 0.0).astype(BF16)

        @pl.when(s < 3)
        def _():
            ones(d, ROWS * d + sub + 32 * half)

        @pl.when(s == 3)
        def _():
            from_c = lax.div(ROWS * d, 256) * 4

            @pl.loop(0, 8)
            def _(i):
                c = from_c + i
                ones(c, lax.div(c, 4) * 256 + lax.rem(c, 4) * 32 + sub + 128 * half)

    loads[0].wait()
    first = ROWS * d - 128 * tile
    row = lax.broadcasted_iota(jnp.int32, (32, 256), 0)
    col = lax.broadcasted_iota(jnp.int32, (32, 256), 1) - first
    pick_low = jnp.where(col == row, 1.0, 0.0).astype(BF16)
    pick_high = jnp.where((col == row + 32) & (row < ROWS - 32), 1.0, 0.0).astype(BF16)
    window = win_v[...]
    both = jnp.concatenate([window, window], axis=0)
    s0_s[...] = jnp.where(low, nt(pick_low, both), nt(pick_high, both)).astype(BF16)

    loads[1].wait()

    @pl.when(s >= 1)
    def _():
        @pl.loop(0, D // 128, unroll=7)
        def _(c):
            part = w_v[:, pl.ds(pl.multiple_of(c * 128, 128), 128)].astype(F32)
            gap = jnp.zeros((R - ROWS, 128), F32)
            wt[pl.ds(pl.multiple_of(c * 128, 128), 128), :] = jnp.concatenate([part, gap, part, gap], axis=0).T

        wt[pl.ds(D, 16), :] = jnp.zeros((16, 128), F32)

        @pl.when(s < 3)
        def _():
            @pl.loop(0, 64, unroll=8)
            def _(c):
                one = wt[pl.ds(pl.multiple_of(c * ROWS, 8), 32), :]
                two = wt[pl.ds(pl.multiple_of(c * ROWS + 32, 8), 32), :]
                le[pl.ds(pl.multiple_of(c * 32, 32), 32), pl.ds(0, 128)] = jnp.where(low, one, two).astype(BF16)

        @pl.when(s == 3)
        def _():
            @pl.loop(0, 56, unroll=8)
            def _(c):
                at = lax.div(c, 4) * 256 + lax.rem(c, 4) * 32
                one = wt[pl.ds(pl.multiple_of(at, 32), 32), :]
                two = wt[pl.ds(pl.multiple_of(at + 128, 32), 32), :]
                le[pl.ds(pl.multiple_of(c * 32, 32), 32), pl.ds(0, 128)] = jnp.where(low, one, two).astype(BF16)

            le[pl.ds(1792, 256), pl.ds(0, 128)] = jnp.zeros((256, 128), BF16)

    pl.semaphore_wait(bar, 17)

    @pl.when(s < 3)
    def _():
        remote(s0_s, s0_r, s0_ss, s0_rs, s + 1, z, p).start()

    for dz in OFFSETS[:-1]:
        pl.semaphore_signal(line, inc=1, device_id=(s, lax.rem(z + dz, 8) * 8 + p), device_id_type=MESH)

    def place(packed):
        turned = pltpu.roll(packed, 64, 1)
        zero = jnp.zeros((32, 128), F32)
        parts = (
            jnp.where(low, packed, zero), jnp.where(low, turned, zero),
            jnp.where(low, zero, turned), jnp.where(low, zero, packed),
        )
        for i, part in enumerate(parts):
            rr[pl.ds(32 * i, 32), :] = part.astype(BF16)
            rr[pl.ds(128 + 32 * i, 32), :] = part.astype(BF16)

    def summed(slot):
        wait_bytes(zb.at[slot], z_rs.at[slot])
        total = zb[slot, 0].astype(F32)
        for i in range(1, 8):
            total = total + zb[slot, i].astype(F32)
        return total

    def spread(k):
        for part, (lo, hi) in enumerate(PARTS):
            for i in range(lo, hi):
                at = pl.ds(pl.multiple_of(lax.rem(z + OFFSETS[i], 8) * 256, 256), 256)
                ob[k, :, i] = jnp.dot(le[at, :], rr[...], preferred_element_type=F32).astype(BF16).reshape(8, 32, 128)
            for j, (a, b) in enumerate(PLANE):
                to_p = plane(a, b)
                span = pl.ds(lo, hi - lo)
                remote(ob.at[k, to_p, span], pb.at[k, j, span], p_ss.at[k], p_rs.at[k, part], s, z, to_p).start()

    def relay(k, midway=None, early=None):
        to_s = jnp.where(s == 3, 2 - k, s + 1)
        slot = jnp.where(s == 3, 1, k)
        for part, (lo, hi) in enumerate(PARTS):
            wait_bytes(pb.at[k, pl.ds(0, hi - lo), pl.ds(0, 7)], p_rs.at[k, part])
            if part == 0 and early is not None:
                early()
            for i in range(lo, hi):
                total = ob[k, p, i].astype(F32)
                for j in range(7):
                    total = total + pb[k, j, i].astype(F32)
                zs[k, i] = total.astype(BF16)
                to_z = lax.rem(z + OFFSETS[i], 8)
                remote(zs.at[k, i], zb.at[slot, z], z_ss.at[k], z_rs.at[slot], to_s, to_z, p).start()
            if part == 2 and midway is not None:
                midway()

    def projected(tokens, both_proj):
        acc[...] = jnp.zeros((TOK, 128), F32)

        @pl.loop(0, 7)
        def _(c):
            at = pl.ds(pl.multiple_of(c * 512, 512), 512)
            acc[...] += nt(tokens[:, at], both_proj[:, at])

    def pass_queries(held, ss, rs):
        for a, b in PLANE:
            to_p = plane(a, b)

            @pl.loop(0, 8)
            def _(i):
                block = held.at[i * 8 + p]
                remote(block, block, ss, rs, s, z, to_p).start()

    def turn_queries(held, rs, turned, blocks=56):
        wait_bytes(held.at[pl.ds(0, blocks)], rs)

        @pl.loop(0, 64)
        def _(c):
            qf[pl.ds(pl.multiple_of(c * 64, 64), 64), :] = held[c].astype(F32)

        for t in range(32):
            turned[:, 128 * t:128 * t + 128] = qf[pl.ds(t, 128, stride=32), :].astype(BF16)

    def go_ahead(to_s):
        pl.semaphore_signal(gate, inc=1, device_id=(to_s, d), device_id_type=MESH)

    def project_inputs():
        for c in loads[3:6]:
            c.wait()
        projected(act_v, pin_v)
        x2[...] = acc[...].astype(BF16)

    position = lax.broadcasted_iota(jnp.int32, (SEQ, 128), 0)

    def sketch(n):
        length = len_ref[n]
        rows = pl.ds(n * SEQ, SEQ)
        g = jnp.where(position < length, acc[rows, :], 0.0).astype(BF16)
        skf[...] = lax.dot_general(g, x2[rows, :], (((0,), (0,)), ((), ())), preferred_element_type=F32)
        pairs = jnp.where(low, skf[pl.ds(0, 32, stride=2), :], skf[pl.ds(1, 32, stride=2), :])
        return pairs / jnp.full((32, 128), length, jnp.int32).astype(F32)

    def lay_flat(n, pairs, to):
        for t in range(32):
            to[pl.ds(n, 1), 128 * t:128 * t + 128] = pairs[t:t + 1, :]

    nearest = (0, 1, 7, 2, 6, 3, 5, 4)

    def gather_line():
        total = summed(1).astype(BF16)

        @pl.when(z < 7)
        def _():
            ag[d] = total
            for dz in OFFSETS[:-1]:
                remote(ag.at[d], ag.at[d], az_ss, az_rs.at[z], s, lax.rem(z + dz, 8), p).start()

    def gather_plane():
        for dz in nearest:
            from_z = lax.rem(z + dz, 8)

            @pl.when(from_z < 7)
            def _():
                block = ag.at[from_z * 8 + p]
                if dz:
                    wait_bytes(block, az_rs.at[from_z])
                for a, b in PLANE:
                    remote(block, block, ap_ss, ap_rs.at[from_z], s, z, plane(a, b)).start()

    def project_tokens():
        wide = lax.broadcasted_iota(jnp.int32, (128, 128), 1) < 64
        acc[...] = jnp.zeros((TOK, 128), F32)
        for group in ((0, 1, 7), (2, 6, 3, 5), (4,)):
            for dz in group:
                from_z = lax.rem(z + dz, 8)

                @pl.when(from_z < 7)
                def _():
                    wait_bytes(ag.at[pl.ds(0, 7)], ap_rs.at[from_z])

            total = acc[...]
            for dz in group:
                from_z = lax.rem(z + dz, 8)
                parts = []
                for c in range(2):
                    piece = ag[pl.ds(from_z * 8 + 4 * c, 4)].reshape(128, 128)
                    zero = jnp.zeros_like(piece)
                    parts += [jnp.where(wide, piece, zero), jnp.where(wide, zero, piece)]
                at = pl.ds(pl.multiple_of(lax.rem(from_z, 7) * 512, 512), 512)
                total = total + jnp.dot(top_v[:, at], jnp.concatenate(parts, axis=0), preferred_element_type=F32)
            acc[...] = total
        acc[...] = acc[...] + pltpu.roll(acc[...], 64, 1)

    @pl.when(s >= 1)
    def _():
        wait_bytes(s0_r, s0_rs)
        place(s0_r[...].astype(F32))

        spread(0)

        @pl.when(s == 1)
        def _():
            go_ahead(0)

    loads[2].wait()
    q32 = qry_v[...].astype(F32)
    for t in range(32):
        qf[pl.ds(t, 1), :] = q32[0:1, 128 * t:128 * t + 128]
        qf[pl.ds(32 + t, 1), :] = q32[1:2, 128 * t:128 * t + 128]
    qb[d] = qf[pl.ds(0, 64), :].astype(BF16)

    @pl.when(s < 2)
    def _():
        for dz in OFFSETS[:-1]:
            remote(qb.at[d], qb.at[d], qz_ss, qz_rs, s, lax.rem(z + dz, 8), p).start()

    def pass_across(first):
        @pl.loop(first, first + 4)
        def _(i):
            block = q3.at[i * 8 + p]
            for a, b in PLANE:
                remote(block, qb.at[i * 8 + p], q3p_ss, qp_rs, 2, z, plane(a, b)).start()

            @pl.when(i != z)
            def _():
                remote(block, qb.at[i * 8 + p], q3p_ss, qp_rs, 2, z, p).start()

    def pass_across_early():
        @pl.when(s == 3)
        def _():
            wait_bytes(q3.at[pl.ds(0, 8)], q3z_rs)
            pass_across(0)

    pl.semaphore_wait(line, 7)

    @pl.when(s == 2)
    def _():
        for dz in OFFSETS:
            remote(qb.at[d], q3.at[d], qz_ss, q3z_rs, 3, lax.rem(z + dz, 8), p).start()

    @pl.when(s == 3)
    def _():
        for dz in OFFSETS:
            remote(qb.at[d], q3.at[d], q3z_ss, q3z_rs, 1, lax.rem(z + dz, 8), p).start()

    @pl.when(s == 2)
    def _():
        place(summed(0))
        spread(1)

    @pl.when(s >= 1)
    def _():
        relay(0, early=pass_across_early)

    @pl.when(s == 2)
    def _():
        relay(1, lambda: go_ahead(3))
        project_inputs()
        gather_line()
        pl.semaphore_wait(gate, 1)

    @pl.when(s == 3)
    def _():
        place(summed(0))
        pl.semaphore_wait(gate, 1)
        spread(1)
        place(summed(1))
        spread(2)
        relay(1)
        relay(2, lambda: go_ahead(2))
        pass_across(4)
        project_inputs()
        for c in loads[6:9]:
            c.wait()
        projected(top_v, pout_v)
        for n in range(2):
            sk_s[pl.ds(32 * n, 32), :] = sketch(n).astype(BF16)
        remote(sk_s, sk_r, sk_ss, sk_rs, 1, z, p).start()

    @pl.when(s < 2)
    def _():
        @pl.when(s == 0)
        def _():
            pl.semaphore_wait(gate, 1)

        wait_bytes(qb.at[pl.ds(0, 7)], qz_rs)
        pass_queries(qb, qp_ss, qp_rs)

        @pl.when(s == 1)
        def _():
            wait_bytes(q3.at[pl.ds(0, 8)], q3z_rs)
            pass_queries(q3, q3p_ss, q3p_rs)

        project_inputs()
        turn_queries(qb, qp_rs, qg)

        @pl.when(s == 1)
        def _():
            turn_queries(q3, q3p_rs, qg3)

        gather_line()

    @pl.when(s < 3)
    def _():
        for c in loads[6:9]:
            c.wait()
        gather_plane()

        project_tokens()

        @pl.when(s == 2)
        def _():
            turn_queries(qb, qp_rs, qg, 63)

        flat[...] = jnp.zeros((16, R * R), F32)
        for n in range(2):
            lay_flat(n, sketch(n), flat)
        ex[s] = nt(flat[...].astype(BF16), qg[...])[0:8]

        @pl.when(s == 1)
        def _():
            wait_bytes(sk_r, sk_rs)
            for n in range(2):
                lay_flat(n, sk_r[pl.ds(32 * n, 32), :].astype(F32), flat)
            ex[s] += nt(flat[...].astype(BF16), qg3[...])[0:8]

        for j in (2, 3, 1):
            remote(ex.at[s], ex.at[s], ex_ss, ex_rs, lax.rem(s + j, 4), z, p).start()

    @pl.when(s < 3)
    def _():
        wait_bytes(ex.at[pl.ds(0, 2)], ex_rs)

    @pl.when(s == 3)
    def _():
        wait_bytes(ex, ex_rs)
    total = ex[0] + ex[1] + ex[2]
    mine = jnp.zeros((8, 32), F32)
    for i in range(4):
        mine = mine + jnp.where(s == i, total[:, 32 * i:32 * i + 32], 0.0)
    out_ref[...] = mine[0:2, :]

    @pl.when(s < 3)
    def _():
        wait_bytes(ex, ex_ss)
        wait_bytes(s0_s, s0_ss)
        wait_bytes(ag.at[pl.ds(0, 49)], ap_ss)

        @pl.when(z < 7)
        def _():
            wait_bytes(ag.at[pl.ds(0, 7)], az_ss)

    @pl.when(s < 2)
    def _():
        wait_bytes(qb.at[pl.ds(0, 7)], qz_ss)
        wait_bytes(qb.at[pl.ds(0, 56)], qp_ss)

    @pl.when(s == 2)
    def _():
        wait_bytes(qb.at[pl.ds(0, 8)], qz_ss)

    @pl.when(s == 1)
    def _():
        wait_bytes(q3.at[pl.ds(0, 56)], q3p_ss)

    @pl.when(s == 3)
    def _():
        wait_bytes(q3.at[pl.ds(0, 8)], q3z_ss)
        wait_bytes(qb.at[pl.ds(0, 63)], q3p_ss)
        wait_bytes(sk_s, sk_ss)

    for k in range(3):
        @pl.when(s > k)
        def _():
            wait_bytes(pb.at[k], p_ss.at[k])
            wait_bytes(zs.at[k], z_ss.at[k])


def local(top_grad, activations, weights, proj_in, proj_out, queries, lengths):
    dma = pltpu.SemaphoreType.DMA
    anywhere = pl.BlockSpec(memory_space=pl.ANY)
    return pl.pallas_call(
        kernel,
        out_shape=jax.ShapeDtypeStruct((2, 32), F32),
        in_specs=[anywhere] * 6 + [pl.BlockSpec(memory_space=pltpu.SMEM)],
        out_specs=pl.BlockSpec(memory_space=pltpu.VMEM),
        scratch_shapes=[
            pltpu.VMEM((ROWS, D), BF16),
            pltpu.VMEM((R, 256), BF16),
            pltpu.VMEM((2, R * R), BF16),
            pltpu.VMEM((2 * R, D), BF16),
            pltpu.VMEM((2 * R, D), BF16),
            pltpu.VMEM((TOK, D), BF16),
            pltpu.VMEM((TOK, D), BF16),
            pltpu.VMEM((D + 16, 128), F32),
            pltpu.VMEM((2048, 256), BF16),
            pltpu.VMEM((256, 128), BF16),
            pltpu.VMEM((32, 128), BF16),
            pltpu.VMEM((32, 128), BF16),
            pltpu.VMEM((3, 8, 8, 32, 128), BF16),
            pltpu.VMEM((3, 7, 8, 32, 128), BF16),
            pltpu.VMEM((3, 8, 32, 128), BF16),
            pltpu.VMEM((2, 8, 32, 128), BF16),
            pltpu.VMEM((64, 32, 128), BF16),
            pltpu.VMEM((64, 64, 128), BF16),
            pltpu.VMEM((64, 64, 128), BF16),
            pltpu.VMEM((4096, 128), F32),
            pltpu.VMEM((128, R * R), BF16),
            pltpu.VMEM((128, R * R), BF16),
            pltpu.VMEM((TOK, 128), F32),
            pltpu.VMEM((TOK, 128), BF16),
            pltpu.VMEM((128, 128), F32),
            pltpu.VMEM((64, 128), BF16),
            pltpu.VMEM((64, 128), BF16),
            pltpu.VMEM((16, R * R), F32),
            pltpu.VMEM((3, 8, 128), F32),
            dma((9,)),
            dma, dma,
            dma((3,)), dma((3, 4)),
            dma((3,)), dma((2,)),
            dma, dma((8,)),
            dma, dma((8,)),
            dma, dma, dma, dma,
            dma, dma, dma, dma, dma, dma,
            dma, dma,
            pltpu.SemaphoreType.REGULAR,
            pltpu.SemaphoreType.REGULAR,
        ],
        compiler_params=pltpu.CompilerParams(
            collective_id=0, has_side_effects=True, vmem_limit_bytes=64 * 2**20 - 2**17
        ),
        name="chain",
    )(top_grad, activations, weights, proj_in, proj_out, queries, lengths) * 0.125


def solution(mesh):
    in_specs = (
        P("dp", None),
        P("section", "dp", None),
        P("section", "dp", None),
        P("section", None, None),
        P("section", None, None),
        P("section", "dp", None),
        P("dp"),
    )
    return jax.shard_map(local, mesh=mesh, in_specs=in_specs, out_specs=P("dp", "section"), check_vma=False)
```

```python
import functools

import jax
import jax.numpy as jnp
from jax import lax
from jax.experimental import pallas as pl
from jax.experimental.pallas import tpu as pltpu
from jax.sharding import PartitionSpec as P

D = 3584
R = 64
ROWS = 56
SEQ = 128
TOK = 256
MESH = pl.DeviceIdType.MESH
F32 = jnp.float32
BF16 = jnp.bfloat16
OFFSETS = (4, 3, 5, 2, 6, 1, 7, 0)
PARTS = ((0, 1), (1, 3), (3, 5), (5, 8))
PLANE = tuple((a, b) for a in (2, 1, 3, 0) for b in (1, 0) if a or b)


def nt(a, b):
    return lax.dot_general(a, b, (((1,), (1,)), ((), ())), preferred_element_type=F32)


def kernel(
    top_ref, act_ref, w_ref, pin_ref, pout_ref, qry_ref, len_ref, out_ref,
    w_v, win_v, qry_v, pin_v, pout_v, act_v, top_v,
    wt, le, l3, lb, lc, rr, rb, r8, s0_s, s0_r, ob, pb, yz, yb, bs, ar_s, ar_r, zs, zb, ag, qb, q3, qf, qg, qg3, acc, x2, skf, sk_s, sk_r, flat, ex,
    ld, s0_ss, s0_rs, p_ss, p_rs, z_ss, z_rs, az_ss, az_rs, ap_ss, ap_rs, qz_ss, qz_rs, qp_ss, qp_rs,
    wa_ss, wa_rs, v_ss, v_rs, y_ss, y_rs, ar_ss, ar_rs, q3z_ss, q3z_rs, q3p_ss, q3p_rs, sk_ss, sk_rs, ex_ss, ex_rs, gate, line,
):
    s = lax.axis_index("section")
    d = lax.axis_index("dp")
    z = lax.div(d, 8)
    p = lax.rem(d, 8)
    y = lax.div(p, 2)
    x = lax.rem(p, 2)
    lane = lax.broadcasted_iota(jnp.int32, (32, 128), 1)
    low = lane < 64

    def plane(a, b):
        return 2 * lax.rem(y + a, 4) + lax.rem(x + b, 2)

    def remote(src, dst, ss, rs, section, at_z, at_p):
        return pltpu.make_async_remote_copy(
            src_ref=src, dst_ref=dst, send_sem=ss, recv_sem=rs,
            device_id=(section, at_z * 8 + at_p), device_id_type=MESH,
        )

    def wait_bytes(ref, sem):
        pltpu.make_async_copy(ref, ref, sem).wait()

    bar = pltpu.get_barrier_semaphore()
    for dz in OFFSETS[:-1]:
        pl.semaphore_signal(bar, inc=1, device_id=(s, lax.rem(z + dz, 8) * 8 + p), device_id_type=MESH)
    for ds in (2, 3, 1):
        pl.semaphore_signal(bar, inc=1, device_id=(lax.rem(s + ds, 4), d), device_id_type=MESH)
    for a, b in PLANE:
        pl.semaphore_signal(bar, inc=1, device_id=(s, z * 8 + plane(a, b)), device_id_type=MESH)

    tile = jnp.minimum(lax.div(ROWS * d, 128), D // 128 - 2)
    loads = [
        pltpu.make_async_copy(pout_ref.at[0, :, pl.ds(pl.multiple_of(tile * 128, 128), 256)], win_v, ld.at[0]),
        pltpu.make_async_copy(w_ref.at[0], w_v, ld.at[1]),
        pltpu.make_async_copy(qry_ref.at[0], qry_v, ld.at[2]),
        pltpu.make_async_copy(act_ref.at[0], act_v, ld.at[3]),
        pltpu.make_async_copy(pin_ref.at[0], pin_v.at[pl.ds(0, R)], ld.at[4]),
        pltpu.make_async_copy(pin_ref.at[0], pin_v.at[pl.ds(R, R)], ld.at[5]),
        pltpu.make_async_copy(top_ref, top_v, ld.at[6]),
        pltpu.make_async_copy(pout_ref.at[0], pout_v.at[pl.ds(0, R)], ld.at[7]),
        pltpu.make_async_copy(pout_ref.at[0], pout_v.at[pl.ds(R, R)], ld.at[8]),
    ]
    for c in loads:
        c.start()

    ag[pl.ds(56, 8)] = jnp.zeros((8, 32, 128), BF16)

    lane_i = jnp.bitwise_and(lane, 63)
    half = jnp.right_shift(lane, 6)
    sub = lax.broadcasted_iota(jnp.int32, (32, 128), 0)

    @pl.when((s == 1) | (s == 2))
    def _():
        le[:, pl.ds(128, 128)] = jnp.zeros((2048, 128), BF16)
        hit = (sub + 32 * half == lane_i) & (lane_i < ROWS)
        le[pl.ds(pl.multiple_of(d * 32, 32), 32), pl.ds(128, 128)] = jnp.where(hit, 1.0, 0.0).astype(BF16)

    loads[0].wait()
    first = ROWS * d - 128 * tile
    row = lax.broadcasted_iota(jnp.int32, (32, 256), 0)
    col = lax.broadcasted_iota(jnp.int32, (32, 256), 1) - first
    pick_low = jnp.where(col == row, 1.0, 0.0).astype(BF16)
    pick_high = jnp.where((col == row + 32) & (row < ROWS - 32), 1.0, 0.0).astype(BF16)
    window = win_v[...]
    both = jnp.concatenate([window, window], axis=0)
    s0_s[...] = jnp.where(low, nt(pick_low, both), nt(pick_high, both)).astype(BF16)

    loads[1].wait()

    @pl.when(s >= 1)
    def _():
        @pl.loop(0, D // 128, unroll=7)
        def _(c):
            part = w_v[:, pl.ds(pl.multiple_of(c * 128, 128), 128)].astype(F32)
            gap = jnp.zeros((R - ROWS, 128), F32)
            wt[pl.ds(pl.multiple_of(c * 128, 128), 128), :] = jnp.concatenate([part, gap, part, gap], axis=0).T

        wt[pl.ds(D, 16), :] = jnp.zeros((16, 128), F32)

        @pl.when(s < 3)
        def _():
            @pl.loop(0, 64, unroll=8)
            def _(c):
                one = wt[pl.ds(pl.multiple_of(c * ROWS, 8), 32), :]
                two = wt[pl.ds(pl.multiple_of(c * ROWS + 32, 8), 32), :]
                le[pl.ds(pl.multiple_of(c * 32, 32), 32), pl.ds(0, 128)] = jnp.where(low, one, two).astype(BF16)

        @pl.when(s == 3)
        def _():
            @pl.loop(0, 7)
            def _(i):
                for j in range(8):
                    at = 512 * i + 256 * (j // 4) + 32 * (j % 4)
                    one = wt[pl.ds(pl.multiple_of(at, 32), 32), :]
                    two = wt[pl.ds(pl.multiple_of(at + 128, 32), 32), :]
                    l3[j, pl.ds(pl.multiple_of(i * 32, 32), 32), :] = jnp.where(low, one, two).astype(BF16)

            l3[:, pl.ds(224, 32), :] = jnp.zeros((8, 32, 128), BF16)

    pl.semaphore_wait(bar, 17)

    @pl.when(s < 3)
    def _():
        remote(s0_s, s0_r, s0_ss, s0_rs, s + 1, z, p).start()

    for dz in OFFSETS[:-1]:
        pl.semaphore_signal(line, inc=1, device_id=(s, lax.rem(z + dz, 8) * 8 + p), device_id_type=MESH)

    def turned_parts(packed):
        turned = pltpu.roll(packed, 64, 1)
        zero = jnp.zeros((32, 128), F32)
        return [
            part.astype(BF16) for part in (
                jnp.where(low, packed, zero), jnp.where(low, turned, zero),
                jnp.where(low, zero, turned), jnp.where(low, zero, packed),
            )
        ]

    def place(packed):
        for i, part in enumerate(turned_parts(packed)):
            rr[pl.ds(32 * i, 32), :] = part
            rr[pl.ds(128 + 32 * i, 32), :] = part

    def summed(slot):
        wait_bytes(zb.at[slot], z_rs.at[slot])
        total = zb[slot, 0].astype(F32)
        for i in range(1, 8):
            total = total + zb[slot, i].astype(F32)
        return total

    def spread():
        for part, (lo, hi) in enumerate(PARTS):
            for i in range(lo, hi):
                at = pl.ds(pl.multiple_of(lax.rem(z + OFFSETS[i], 8) * 256, 256), 256)
                ob[:, i] = jnp.dot(le[at, :], rr[...], preferred_element_type=F32).astype(BF16).reshape(8, 32, 128)
            for j, (a, b) in enumerate(PLANE):
                to_p = plane(a, b)
                span = pl.ds(lo, hi - lo)
                remote(ob.at[to_p, span], pb.at[j, span], p_ss, p_rs.at[part], s, z, to_p).start()

    def relay():
        for part, (lo, hi) in enumerate(PARTS):
            wait_bytes(pb.at[pl.ds(0, hi - lo), pl.ds(0, 7)], p_rs.at[part])
            for i in range(lo, hi):
                total = ob[p, i].astype(F32)
                for j in range(7):
                    total = total + pb[j, i].astype(F32)
                zs[0, i] = total.astype(BF16)
                to_z = lax.rem(z + OFFSETS[i], 8)
                remote(zs.at[0, i], zb.at[0, z], z_ss.at[0], z_rs.at[0], s + 1, to_z, p).start()

    def send_columns():
        for dz in OFFSETS[:-1]:
            to_z = lax.rem(z + dz, 8)
            block = le.at[pl.ds(pl.multiple_of(to_z * 256, 256), 256), pl.ds(0, 128)]
            remote(block, lb.at[z], wa_ss, wa_rs, s, to_z, p).start()
        lb[z] = le[pl.ds(pl.multiple_of(z * 256, 256), 256), pl.ds(0, 128)]

    def line_product():
        for dz in nearest:
            from_z = lax.rem(z + dz, 8)
            if dz:
                wait_bytes(yz.at[from_z], v_rs.at[from_z])
            for i, part in enumerate(turned_parts(yz[from_z].astype(F32))):
                rb[from_z, pl.ds(32 * i, 32), :] = part
        wait_bytes(l3.at[pl.ds(0, 7)], wa_rs)
        total = jnp.zeros((TOK, 128), F32)
        for i in range(4):
            left = jnp.concatenate([lb[2 * i], lb[2 * i + 1]], axis=1)
            total = total + jnp.dot(left, rb[pl.ds(2 * i, 2)].reshape(256, 128), preferred_element_type=F32)
        bs[...] = total.reshape(8, 32, 128)
        bs[p] += yz[z].astype(F32)
        ar_s[...] = bs[...].reshape(TOK, 128).astype(BF16)
        for a, b in PLANE + ((0, 0),):
            remote(ar_s, ar_r.at[p], ar_ss, ar_rs, 3, z, plane(a, b)).start()

    def plane_product(k):
        total = jnp.zeros((TOK, 128), F32)
        for j in range(8):
            for i, part in enumerate(turned_parts(yb[k, j].astype(F32))):
                r8[j, pl.ds(32 * i, 32), :] = part
                r8[j, pl.ds(128 + 32 * i, 32), :] = part
        for j in range(8):
            total = total + jnp.dot(lc[j], r8[j], preferred_element_type=F32)
        zs[k] = total.astype(BF16).reshape(8, 32, 128)
        for dz in OFFSETS:
            to_z = lax.rem(z + dz, 8)
            remote(zs.at[k, to_z], zb.at[1, z], z_ss.at[k], z_rs.at[1], 2 - k, to_z, p).start()

    def share_plane(k):
        for a, b in PLANE:
            remote(yb.at[k, p], yb.at[k, p], y_ss.at[k], y_rs.at[k], s, z, plane(a, b)).start()

    def projected(tokens, both_proj):
        acc[...] = jnp.zeros((TOK, 128), F32)

        @pl.loop(0, 7)
        def _(c):
            at = pl.ds(pl.multiple_of(c * 512, 512), 512)
            acc[...] += nt(tokens[:, at], both_proj[:, at])

    def pass_queries(held, ss, rs):
        for a, b in PLANE:
            to_p = plane(a, b)

            @pl.loop(0, 8)
            def _(i):
                block = held.at[i * 8 + p]
                remote(block, block, ss, rs, s, z, to_p).start()

    def turn_queries(held, rs, turned, blocks=56):
        wait_bytes(held.at[pl.ds(0, blocks)], rs)

        @pl.loop(0, 64)
        def _(c):
            qf[pl.ds(pl.multiple_of(c * 64, 64), 64), :] = held[c].astype(F32)

        for t in range(32):
            turned[:, 128 * t:128 * t + 128] = qf[pl.ds(t, 128, stride=32), :].astype(BF16)

    def go_ahead(to_s):
        pl.semaphore_signal(gate, inc=1, device_id=(to_s, d), device_id_type=MESH)

    def project_inputs():
        for c in loads[3:6]:
            c.wait()
        projected(act_v, pin_v)
        x2[...] = acc[...].astype(BF16)

    position = lax.broadcasted_iota(jnp.int32, (SEQ, 128), 0)

    def sketch(n):
        length = len_ref[n]
        rows = pl.ds(n * SEQ, SEQ)
        g = jnp.where(position < length, acc[rows, :], 0.0).astype(BF16)
        skf[...] = lax.dot_general(g, x2[rows, :], (((0,), (0,)), ((), ())), preferred_element_type=F32)
        pairs = jnp.where(low, skf[pl.ds(0, 32, stride=2), :], skf[pl.ds(1, 32, stride=2), :])
        return pairs / jnp.full((32, 128), length, jnp.int32).astype(F32)

    def lay_flat(n, pairs, to):
        for t in range(32):
            to[pl.ds(n, 1), 128 * t:128 * t + 128] = pairs[t:t + 1, :]

    nearest = (0, 1, 7, 2, 6, 3, 5, 4)

    def gather_line():
        total = summed(1).astype(BF16)

        @pl.when(z < 7)
        def _():
            ag[d] = total
            for dz in OFFSETS[:-1]:
                remote(ag.at[d], ag.at[d], az_ss, az_rs.at[z], s, lax.rem(z + dz, 8), p).start()

    def gather_plane():
        for dz in nearest:
            from_z = lax.rem(z + dz, 8)

            @pl.when(from_z < 7)
            def _():
                block = ag.at[from_z * 8 + p]
                if dz:
                    wait_bytes(block, az_rs.at[from_z])
                for a, b in PLANE:
                    remote(block, block, ap_ss, ap_rs.at[from_z], s, z, plane(a, b)).start()

    def project_tokens():
        wide = lax.broadcasted_iota(jnp.int32, (128, 128), 1) < 64
        acc[...] = jnp.zeros((TOK, 128), F32)
        for group in ((0, 1, 7), (2, 6, 3, 5), (4,)):
            for dz in group:
                from_z = lax.rem(z + dz, 8)

                @pl.when(from_z < 7)
                def _():
                    wait_bytes(ag.at[pl.ds(0, 7)], ap_rs.at[from_z])

            total = acc[...]
            for dz in group:
                from_z = lax.rem(z + dz, 8)
                parts = []
                for c in range(2):
                    piece = ag[pl.ds(from_z * 8 + 4 * c, 4)].reshape(128, 128)
                    zero = jnp.zeros_like(piece)
                    parts += [jnp.where(wide, piece, zero), jnp.where(wide, zero, piece)]
                at = pl.ds(pl.multiple_of(lax.rem(from_z, 7) * 512, 512), 512)
                total = total + jnp.dot(top_v[:, at], jnp.concatenate(parts, axis=0), preferred_element_type=F32)
            acc[...] = total
        acc[...] = acc[...] + pltpu.roll(acc[...], 64, 1)

    @pl.when(s == 2)
    def _():
        send_columns()

    @pl.when((s == 1) | (s == 2))
    def _():
        wait_bytes(s0_r, s0_rs)
        place(s0_r[...].astype(F32))
        spread()

        @pl.when(s == 1)
        def _():
            go_ahead(0)

    @pl.when(s == 3)
    def _():
        for a, b in PLANE:
            to_p = plane(a, b)
            remote(l3.at[to_p], lc.at[p, :, pl.ds(0, 128)], wa_ss, wa_rs, s, z, to_p).start()
        lc[p, :, 0:128] = l3[p]
        wait_bytes(s0_r, s0_rs)
        yb[0, p] = s0_r[...]
        share_plane(0)

        @pl.loop(0, 8)
        def _(j):
            for i in range(8):
                at = 512 * i + lax.div(p, 4) * 256 + lax.rem(p, 4) * 32 + sub + 128 * half
                hit = (at - ROWS * (8 * z + j) == lane_i) & (lane_i < ROWS)
                lc[j, 32 * i:32 * i + 32, 128:256] = jnp.where(hit, 1.0, 0.0).astype(BF16)

    loads[2].wait()
    q32 = qry_v[...].astype(F32)
    for t in range(32):
        qf[pl.ds(t, 1), :] = q32[0:1, 128 * t:128 * t + 128]
        qf[pl.ds(32 + t, 1), :] = q32[1:2, 128 * t:128 * t + 128]
    qb[d] = qf[pl.ds(0, 64), :].astype(BF16)

    @pl.when(s < 2)
    def _():
        for dz in OFFSETS[:-1]:
            remote(qb.at[d], qb.at[d], qz_ss, qz_rs, s, lax.rem(z + dz, 8), p).start()

    def pass_across(first):
        @pl.loop(first, first + 4)
        def _(i):
            block = q3.at[i * 8 + p]
            for a, b in PLANE:
                remote(block, qb.at[i * 8 + p], q3p_ss, qp_rs, 2, z, plane(a, b)).start()

            @pl.when(i != z)
            def _():
                remote(block, qb.at[i * 8 + p], q3p_ss, qp_rs, 2, z, p).start()

    pl.semaphore_wait(line, 7)

    @pl.when(s == 2)
    def _():
        for dz in OFFSETS:
            remote(qb.at[d], q3.at[d], qz_ss, q3z_rs, 3, lax.rem(z + dz, 8), p).start()

    @pl.when(s == 3)
    def _():
        for dz in OFFSETS:
            remote(qb.at[d], q3.at[d], q3z_ss, q3z_rs, 1, lax.rem(z + dz, 8), p).start()

    @pl.when(s == 2)
    def _():
        yz[z] = summed(0).astype(BF16)
        for dz in OFFSETS[:-1]:
            remote(yz.at[z], yz.at[z], v_ss, v_rs.at[z], s, lax.rem(z + dz, 8), p).start()

    @pl.when((s == 1) | (s == 2))
    def _():
        relay()

    @pl.when(s == 2)
    def _():
        line_product()
        project_inputs()
        gather_line()
        pl.semaphore_wait(gate, 1)

    @pl.when(s == 3)
    def _():
        wait_bytes(l3.at[pl.ds(0, 7)], wa_rs)
        wait_bytes(yb.at[0, pl.ds(0, 7)], y_rs.at[0])
        plane_product(0)
        wait_bytes(q3.at[pl.ds(0, 8)], q3z_rs)
        pass_across(0)
        yb[1, p] = summed(0).astype(BF16)
        share_plane(1)
        wait_bytes(yb.at[1, pl.ds(0, 7)], y_rs.at[1])
        plane_product(1)
        wait_bytes(ar_r, ar_rs)
        total = ar_r[0].astype(F32)
        for i in range(1, 8):
            total = total + ar_r[i].astype(F32)
        yb[2] = total.reshape(8, 32, 128).astype(BF16)
        plane_product(2)
        go_ahead(2)
        pass_across(4)
        project_inputs()
        for c in loads[6:9]:
            c.wait()
        projected(top_v, pout_v)
        for n in range(2):
            sk_s[pl.ds(32 * n, 32), :] = sketch(n).astype(BF16)
        remote(sk_s, sk_r, sk_ss, sk_rs, 1, z, p).start()

    @pl.when(s < 2)
    def _():
        @pl.when(s == 0)
        def _():
            pl.semaphore_wait(gate, 1)

        wait_bytes(qb.at[pl.ds(0, 7)], qz_rs)
        pass_queries(qb, qp_ss, qp_rs)

        @pl.when(s == 1)
        def _():
            wait_bytes(q3.at[pl.ds(0, 8)], q3z_rs)
            pass_queries(q3, q3p_ss, q3p_rs)

        project_inputs()
        turn_queries(qb, qp_rs, qg)

        gather_line()

    @pl.when(s < 3)
    def _():
        for c in loads[6:9]:
            c.wait()
        gather_plane()

        @pl.when(s == 1)
        def _():
            turn_queries(q3, q3p_rs, qg3)

        project_tokens()

        @pl.when(s == 2)
        def _():
            turn_queries(qb, qp_rs, qg, 63)

        flat[...] = jnp.zeros((16, R * R), F32)
        for n in range(2):
            lay_flat(n, sketch(n), flat)
        ex[s] = nt(flat[...].astype(BF16), qg[...])[0:8]

        @pl.when(s == 1)
        def _():
            wait_bytes(sk_r, sk_rs)
            for n in range(2):
                lay_flat(n, sk_r[pl.ds(32 * n, 32), :].astype(F32), flat)
            ex[s] += nt(flat[...].astype(BF16), qg3[...])[0:8]

        for j in (2, 3, 1):
            remote(ex.at[s], ex.at[s], ex_ss, ex_rs, lax.rem(s + j, 4), z, p).start()

    @pl.when(s < 3)
    def _():
        wait_bytes(ex.at[pl.ds(0, 2)], ex_rs)

    @pl.when(s == 3)
    def _():
        wait_bytes(ex, ex_rs)
    total = ex[0] + ex[1] + ex[2]
    mine = jnp.zeros((8, 32), F32)
    for i in range(4):
        mine = mine + jnp.where(s == i, total[:, 32 * i:32 * i + 32], 0.0)
    out_ref[...] = mine[0:2, :]

    @pl.when(s < 3)
    def _():
        wait_bytes(ex, ex_ss)
        wait_bytes(s0_s, s0_ss)
        wait_bytes(ag.at[pl.ds(0, 49)], ap_ss)

        @pl.when(z < 7)
        def _():
            wait_bytes(ag.at[pl.ds(0, 7)], az_ss)

    @pl.when(s < 2)
    def _():
        wait_bytes(qb.at[pl.ds(0, 7)], qz_ss)
        wait_bytes(qb.at[pl.ds(0, 56)], qp_ss)

    @pl.when(s == 2)
    def _():
        wait_bytes(qb.at[pl.ds(0, 8)], qz_ss)

    @pl.when(s == 1)
    def _():
        wait_bytes(q3.at[pl.ds(0, 56)], q3p_ss)

    @pl.when(s == 3)
    def _():
        wait_bytes(q3.at[pl.ds(0, 8)], q3z_ss)
        wait_bytes(qb.at[pl.ds(0, 63)], q3p_ss)
        wait_bytes(sk_s, sk_ss)

    @pl.when((s == 1) | (s == 2))
    def _():
        wait_bytes(pb, p_ss)
        wait_bytes(zs.at[0], z_ss.at[0])

    @pl.when(s >= 2)
    def _():
        wait_bytes(l3.at[pl.ds(0, 7)], wa_ss)

    @pl.when(s == 2)
    def _():
        wait_bytes(yz.at[pl.ds(0, 7)], v_ss)
        wait_bytes(ar_r, ar_ss)

    @pl.when(s == 3)
    def _():
        for k in range(3):
            wait_bytes(zs.at[k], z_ss.at[k])
        for k in range(2):
            wait_bytes(yb.at[k, pl.ds(0, 7)], y_ss.at[k])


def local(top_grad, activations, weights, proj_in, proj_out, queries, lengths):
    dma = pltpu.SemaphoreType.DMA
    anywhere = pl.BlockSpec(memory_space=pl.ANY)
    return pl.pallas_call(
        kernel,
        out_shape=jax.ShapeDtypeStruct((2, 32), F32),
        in_specs=[anywhere] * 6 + [pl.BlockSpec(memory_space=pltpu.SMEM)],
        out_specs=pl.BlockSpec(memory_space=pltpu.VMEM),
        scratch_shapes=[
            pltpu.VMEM((ROWS, D), BF16),
            pltpu.VMEM((R, 256), BF16),
            pltpu.VMEM((2, R * R), BF16),
            pltpu.VMEM((2 * R, D), BF16),
            pltpu.VMEM((2 * R, D), BF16),
            pltpu.VMEM((TOK, D), BF16),
            pltpu.VMEM((TOK, D), BF16),
            pltpu.VMEM((D + 16, 128), F32),
            pltpu.VMEM((2048, 256), BF16),
            pltpu.VMEM((8, 256, 128), BF16),
            pltpu.VMEM((8, 256, 128), BF16),
            pltpu.VMEM((8, 256, 256), BF16),
            pltpu.VMEM((256, 128), BF16),
            pltpu.VMEM((8, 128, 128), BF16),
            pltpu.VMEM((8, 256, 128), BF16),
            pltpu.VMEM((32, 128), BF16),
            pltpu.VMEM((32, 128), BF16),
            pltpu.VMEM((8, 8, 32, 128), BF16),
            pltpu.VMEM((7, 8, 32, 128), BF16),
            pltpu.VMEM((8, 32, 128), BF16),
            pltpu.VMEM((3, 8, 32, 128), BF16),
            pltpu.VMEM((8, 32, 128), F32),
            pltpu.VMEM((TOK, 128), BF16),
            pltpu.VMEM((8, TOK, 128), BF16),
            pltpu.VMEM((3, 8, 32, 128), BF16),
            pltpu.VMEM((2, 8, 32, 128), BF16),
            pltpu.VMEM((64, 32, 128), BF16),
            pltpu.VMEM((64, 64, 128), BF16),
            pltpu.VMEM((64, 64, 128), BF16),
            pltpu.VMEM((4096, 128), F32),
            pltpu.VMEM((128, R * R), BF16),
            pltpu.VMEM((128, R * R), BF16),
            pltpu.VMEM((TOK, 128), F32),
            pltpu.VMEM((TOK, 128), BF16),
            pltpu.VMEM((128, 128), F32),
            pltpu.VMEM((64, 128), BF16),
            pltpu.VMEM((64, 128), BF16),
            pltpu.VMEM((16, R * R), F32),
            pltpu.VMEM((3, 8, 128), F32),
            dma((9,)),
            dma, dma,
            dma, dma((4,)),
            dma((3,)), dma((2,)),
            dma, dma((8,)),
            dma, dma((8,)),
            dma, dma, dma, dma,
            dma, dma, dma, dma((8,)), dma((2,)), dma((2,)), dma, dma,
            dma, dma, dma, dma, dma, dma,
            dma, dma,
            pltpu.SemaphoreType.REGULAR,
            pltpu.SemaphoreType.REGULAR,
        ],
        compiler_params=pltpu.CompilerParams(
            collective_id=0, has_side_effects=True, vmem_limit_bytes=64 * 2**20 - 2**17
        ),
        name="chain",
    )(top_grad, activations, weights, proj_in, proj_out, queries, lengths) * 0.125


def solution(mesh):
    in_specs = (
        P("dp", None),
        P("section", "dp", None),
        P("section", "dp", None),
        P("section", None, None),
        P("section", None, None),
        P("section", "dp", None),
        P("dp"),
    )
    return jax.shard_map(local, mesh=mesh, in_specs=in_specs, out_specs=P("dp", "section"), check_vma=False)
```

```python
import functools

import jax
import jax.numpy as jnp
from jax import lax
from jax.experimental import pallas as pl
from jax.experimental.pallas import tpu as pltpu
from jax.sharding import PartitionSpec as P

D = 3584
R = 64
ROWS = 56
SEQ = 128
TOK = 256
MESH = pl.DeviceIdType.MESH
F32 = jnp.float32
BF16 = jnp.bfloat16
OFFSETS = (4, 3, 5, 2, 6, 1, 7, 0)
PARTS = ((0, 1), (1, 3), (3, 5), (5, 8))
PLANE = tuple((a, b) for a in (2, 1, 3, 0) for b in (1, 0) if a or b)


def nt(a, b):
    return lax.dot_general(a, b, (((1,), (1,)), ((), ())), preferred_element_type=F32)


def kernel(
    top_ref, act_ref, w_ref, pin_ref, pout_ref, qry_ref, len_ref, out_ref,
    w_v, win_v, qry_v, pin_v, pout_v, act_v, top_v,
    wt, le, l3, lb, lc, rr, rb, r8, s0_s, s0_r, ob, pb, yz, yb, bs, ar_s, ar_r, zs, zb, ag, qown, qb, q3, qf, qg, qg3, acc, x2, xr, skf, sk_s, sk_r, flat, ex,
    ld, s0_ss, s0_rs, p_ss, p_rs, z_ss, z_rs, az_ss, az_rs, ap_ss, ap_rs, qz_ss, qz_rs, qp_ss, qp_rs,
    wa_ss, wa_rs, v_ss, v_rs, y_ss, y_rs, ar_ss, ar_rs, q3z_rs, q3p_ss, q3p_rs, q3v_ss, q3v_rs, x_ss, x_rs, sk_ss, sk_rs, ex_ss, ex_rs, gate, line,
):
    s = lax.axis_index("section")
    d = lax.axis_index("dp")
    z = lax.div(d, 8)
    p = lax.rem(d, 8)
    y = lax.div(p, 2)
    x = lax.rem(p, 2)
    lane = lax.broadcasted_iota(jnp.int32, (32, 128), 1)
    low = lane < 64

    def plane(a, b):
        return 2 * lax.rem(y + a, 4) + lax.rem(x + b, 2)

    def remote(src, dst, ss, rs, section, at_z, at_p):
        return pltpu.make_async_remote_copy(
            src_ref=src, dst_ref=dst, send_sem=ss, recv_sem=rs,
            device_id=(section, at_z * 8 + at_p), device_id_type=MESH,
        )

    def wait_bytes(ref, sem):
        pltpu.make_async_copy(ref, ref, sem).wait()

    bar = pltpu.get_barrier_semaphore()
    for dz in OFFSETS[:-1]:
        pl.semaphore_signal(bar, inc=1, device_id=(s, lax.rem(z + dz, 8) * 8 + p), device_id_type=MESH)
    for ds in (2, 3, 1):
        pl.semaphore_signal(bar, inc=1, device_id=(lax.rem(s + ds, 4), d), device_id_type=MESH)
    for a, b in PLANE:
        pl.semaphore_signal(bar, inc=1, device_id=(s, z * 8 + plane(a, b)), device_id_type=MESH)

    tile = jnp.minimum(lax.div(ROWS * d, 128), D // 128 - 2)
    loads = [
        pltpu.make_async_copy(pout_ref.at[0, :, pl.ds(pl.multiple_of(tile * 128, 128), 256)], win_v, ld.at[0]),
        pltpu.make_async_copy(w_ref.at[0], w_v, ld.at[1]),
        pltpu.make_async_copy(qry_ref.at[0], qry_v, ld.at[2]),
        pltpu.make_async_copy(act_ref.at[0], act_v, ld.at[3]),
        pltpu.make_async_copy(pin_ref.at[0], pin_v.at[pl.ds(0, R)], ld.at[4]),
        pltpu.make_async_copy(pin_ref.at[0], pin_v.at[pl.ds(R, R)], ld.at[5]),
        pltpu.make_async_copy(top_ref, top_v, ld.at[6]),
        pltpu.make_async_copy(pout_ref.at[0], pout_v.at[pl.ds(0, R)], ld.at[7]),
        pltpu.make_async_copy(pout_ref.at[0], pout_v.at[pl.ds(R, R)], ld.at[8]),
    ]
    for c in loads:
        c.start()

    ag[pl.ds(56, 8)] = jnp.zeros((8, 32, 128), BF16)

    lane_i = jnp.bitwise_and(lane, 63)
    half = jnp.right_shift(lane, 6)
    sub = lax.broadcasted_iota(jnp.int32, (32, 128), 0)

    @pl.when((s == 1) | (s == 2))
    def _():
        le[:, pl.ds(128, 128)] = jnp.zeros((2048, 128), BF16)
        hit = (sub + 32 * half == lane_i) & (lane_i < ROWS)
        le[pl.ds(pl.multiple_of(d * 32, 32), 32), pl.ds(128, 128)] = jnp.where(hit, 1.0, 0.0).astype(BF16)

    loads[0].wait()
    first = ROWS * d - 128 * tile
    row = lax.broadcasted_iota(jnp.int32, (32, 256), 0)
    col = lax.broadcasted_iota(jnp.int32, (32, 256), 1) - first
    pick_low = jnp.where(col == row, 1.0, 0.0).astype(BF16)
    pick_high = jnp.where((col == row + 32) & (row < ROWS - 32), 1.0, 0.0).astype(BF16)
    window = win_v[...]
    both = jnp.concatenate([window, window], axis=0)
    s0_s[...] = jnp.where(low, nt(pick_low, both), nt(pick_high, both)).astype(BF16)

    loads[1].wait()

    @pl.when(s >= 1)
    def _():
        @pl.loop(0, D // 128, unroll=7)
        def _(c):
            part = w_v[:, pl.ds(pl.multiple_of(c * 128, 128), 128)].astype(F32)
            gap = jnp.zeros((R - ROWS, 128), F32)
            wt[pl.ds(pl.multiple_of(c * 128, 128), 128), :] = jnp.concatenate([part, gap, part, gap], axis=0).T

        wt[pl.ds(D, 16), :] = jnp.zeros((16, 128), F32)

        @pl.when(s < 3)
        def _():
            @pl.loop(0, 64, unroll=8)
            def _(c):
                one = wt[pl.ds(pl.multiple_of(c * ROWS, 8), 32), :]
                two = wt[pl.ds(pl.multiple_of(c * ROWS + 32, 8), 32), :]
                le[pl.ds(pl.multiple_of(c * 32, 32), 32), pl.ds(0, 128)] = jnp.where(low, one, two).astype(BF16)

        @pl.when(s == 3)
        def _():
            @pl.loop(0, 7)
            def _(i):
                for j in range(8):
                    at = 512 * i + 256 * (j // 4) + 32 * (j % 4)
                    one = wt[pl.ds(pl.multiple_of(at, 32), 32), :]
                    two = wt[pl.ds(pl.multiple_of(at + 128, 32), 32), :]
                    l3[j, pl.ds(pl.multiple_of(i * 32, 32), 32), :] = jnp.where(low, one, two).astype(BF16)

            l3[:, pl.ds(224, 32), :] = jnp.zeros((8, 32, 128), BF16)

    pl.semaphore_wait(bar, 17)

    @pl.when(s < 3)
    def _():
        remote(s0_s, s0_r, s0_ss, s0_rs, s + 1, z, p).start()

    for dz in OFFSETS[:-1]:
        pl.semaphore_signal(line, inc=1, device_id=(s, lax.rem(z + dz, 8) * 8 + p), device_id_type=MESH)

    def turned_parts(packed):
        turned = pltpu.roll(packed, 64, 1)
        zero = jnp.zeros((32, 128), F32)
        return [
            part.astype(BF16) for part in (
                jnp.where(low, packed, zero), jnp.where(low, turned, zero),
                jnp.where(low, zero, turned), jnp.where(low, zero, packed),
            )
        ]

    def place(packed):
        for i, part in enumerate(turned_parts(packed)):
            rr[pl.ds(32 * i, 32), :] = part
            rr[pl.ds(128 + 32 * i, 32), :] = part

    def summed(slot, count=8):
        wait_bytes(zb.at[slot, pl.ds(0, count)], z_rs.at[slot])
        total = zb[slot, 0].astype(F32)
        for i in range(1, 8):
            total = total + zb[slot, i].astype(F32)
        return total

    def spread():
        for part, (lo, hi) in enumerate(PARTS):
            for i in range(lo, hi):
                at = pl.ds(pl.multiple_of(lax.rem(z + OFFSETS[i], 8) * 256, 256), 256)
                ob[:, i] = jnp.dot(le[at, :], rr[...], preferred_element_type=F32).astype(BF16).reshape(8, 32, 128)
            for j, (a, b) in enumerate(PLANE):
                to_p = plane(a, b)
                span = pl.ds(lo, hi - lo)
                remote(ob.at[to_p, span], pb.at[j, span], p_ss, p_rs.at[part], s, z, to_p).start()

    def relay():
        for part, (lo, hi) in enumerate(PARTS):
            wait_bytes(pb.at[pl.ds(0, hi - lo), pl.ds(0, 7)], p_rs.at[part])
            for i in range(lo, hi):
                total = ob[p, i].astype(F32)
                for j in range(7):
                    total = total + pb[j, i].astype(F32)
                zs[0, i] = total.astype(BF16)
                to_z = lax.rem(z + OFFSETS[i], 8)
                remote(zs.at[0, i], zb.at[0, z], z_ss.at[0], z_rs.at[0], s + 1, to_z, p).start()

    def send_columns():
        for dz in OFFSETS[:-1]:
            to_z = lax.rem(z + dz, 8)
            block = le.at[pl.ds(pl.multiple_of(to_z * 256, 256), 256), pl.ds(0, 128)]
            remote(block, lb.at[z], wa_ss, wa_rs, s, to_z, p).start()
        lb[z] = le[pl.ds(pl.multiple_of(z * 256, 256), 256), pl.ds(0, 128)]

    def line_product():
        for dz in nearest:
            from_z = lax.rem(z + dz, 8)
            if dz:
                wait_bytes(yz.at[from_z], v_rs.at[from_z])
            for i, part in enumerate(turned_parts(yz[from_z].astype(F32))):
                rb[from_z, pl.ds(32 * i, 32), :] = part
        wait_bytes(l3.at[pl.ds(0, 7)], wa_rs)
        total = jnp.zeros((TOK, 128), F32)
        for i in range(4):
            left = jnp.concatenate([lb[2 * i], lb[2 * i + 1]], axis=1)
            total = total + jnp.dot(left, rb[pl.ds(2 * i, 2)].reshape(256, 128), preferred_element_type=F32)
        bs[...] = total.reshape(8, 32, 128)
        bs[p] += yz[z].astype(F32)
        ar_s[...] = bs[...].reshape(TOK, 128).astype(BF16)
        for a, b in PLANE + ((0, 0),):
            remote(ar_s, ar_r.at[p], ar_ss, ar_rs, 3, z, plane(a, b)).start()

    def plane_product(k):
        total = jnp.zeros((TOK, 128), F32)
        for j in range(8):
            for i, part in enumerate(turned_parts(yb[k, j].astype(F32))):
                r8[j, pl.ds(32 * i, 32), :] = part
                r8[j, pl.ds(128 + 32 * i, 32), :] = part
        for j in range(8):
            total = total + jnp.dot(lc[j], r8[j], preferred_element_type=F32)
        zs[k] = total.astype(BF16).reshape(8, 32, 128)
        for dz in OFFSETS:
            to_z = lax.rem(z + dz, 8)
            if k == 2 and dz == 0:
                zb[1, z] = zs[k, z]
            else:
                remote(zs.at[k, to_z], zb.at[1, z], z_ss.at[k], z_rs.at[1], (0, 1, 3)[k], to_z, p).start()

    def share_plane(k):
        for a, b in PLANE:
            remote(yb.at[k, p], yb.at[k, p], y_ss.at[k], y_rs.at[k], s, z, plane(a, b)).start()

    def projected(tokens, both_proj):
        acc[...] = jnp.zeros((TOK, 128), F32)

        @pl.loop(0, 7)
        def _(c):
            at = pl.ds(pl.multiple_of(c * 512, 512), 512)
            acc[...] += nt(tokens[:, at], both_proj[:, at])

    def pass_queries(held, ss, rs, first=0, count=8):
        for a, b in PLANE:
            to_p = plane(a, b)

            @pl.loop(first, first + count)
            def _(i):
                block = held.at[i * 8 + p]
                remote(block, block, ss, rs, s, z, to_p).start()

    def turn_queries(held, turned, first=0, count=8):
        @pl.loop(8 * first, 8 * (first + count))
        def _(c):
            qf[pl.ds(pl.multiple_of(c * 64, 64), 64), :] = held[c].astype(F32)

        for t in range(32):
            rows = qf[pl.ds(512 * first + t, 16 * count, stride=32), :]
            turned[128 * t:128 * t + 128, 16 * first:16 * (first + count)] = rows.T.astype(BF16)

    def scored(turned):
        return jnp.dot(flat[...].astype(BF16), turned[...], preferred_element_type=F32)[0:8]

    def wait_queries(held, rs, blocks=56):
        wait_bytes(held.at[pl.ds(0, blocks)], rs)

    def go_ahead(to_s):
        pl.semaphore_signal(gate, inc=1, device_id=(to_s, d), device_id_type=MESH)

    def project_inputs():
        for c in loads[3:6]:
            c.wait()
        projected(act_v, pin_v)
        x2[...] = acc[...].astype(BF16)

    position = lax.broadcasted_iota(jnp.int32, (SEQ, 128), 0)

    def sketch(n, held):
        length = len_ref[n]
        rows = pl.ds(n * SEQ, SEQ)
        g = jnp.where(position < length, acc[rows, :], 0.0).astype(BF16)
        skf[...] = lax.dot_general(g, held[rows, :], (((0,), (0,)), ((), ())), preferred_element_type=F32)
        pairs = jnp.where(low, skf[pl.ds(0, 32, stride=2), :], skf[pl.ds(1, 32, stride=2), :])
        return pairs / jnp.full((32, 128), length, jnp.int32).astype(F32)

    def lay_flat(n, pairs, to):
        for t in range(32):
            to[pl.ds(n, 1), 128 * t:128 * t + 128] = pairs[t:t + 1, :]

    slot = jnp.minimum(s, 2)
    nearest = (0, 1, 7, 2, 6, 3, 5, 4)

    def gather_line(count=8):
        total = summed(1, count).astype(BF16)

        @pl.when(z < 7)
        def _():
            ag[d] = total
            for dz in OFFSETS[:-1]:
                remote(ag.at[d], ag.at[d], az_ss, az_rs.at[z], s, lax.rem(z + dz, 8), p).start()

    def gather_plane():
        for dz in nearest:
            from_z = lax.rem(z + dz, 8)

            @pl.when(from_z < 7)
            def _():
                block = ag.at[from_z * 8 + p]
                if dz:
                    wait_bytes(block, az_rs.at[from_z])
                for a, b in PLANE:
                    remote(block, block, ap_ss, ap_rs.at[from_z], s, z, plane(a, b)).start()

    def project_tokens():
        wide = lax.broadcasted_iota(jnp.int32, (128, 128), 1) < 64
        acc[...] = jnp.zeros((TOK, 128), F32)
        for group in ((0, 1, 7), (2, 6), (3, 5), (4,)):
            for dz in group:
                from_z = lax.rem(z + dz, 8)

                @pl.when(from_z < 7)
                def _():
                    wait_bytes(ag.at[pl.ds(0, 7)], ap_rs.at[from_z])

            total = acc[...]
            for dz in group:
                from_z = lax.rem(z + dz, 8)
                parts = []
                for c in range(2):
                    piece = ag[pl.ds(from_z * 8 + 4 * c, 4)].reshape(128, 128)
                    zero = jnp.zeros_like(piece)
                    parts += [jnp.where(wide, piece, zero), jnp.where(wide, zero, piece)]
                at = pl.ds(pl.multiple_of(lax.rem(from_z, 7) * 512, 512), 512)
                total = total + jnp.dot(top_v[:, at], jnp.concatenate(parts, axis=0), preferred_element_type=F32)
            acc[...] = total
        acc[...] = acc[...] + pltpu.roll(acc[...], 64, 1)

    @pl.when(s == 2)
    def _():
        send_columns()

    @pl.when((s == 1) | (s == 2))
    def _():
        wait_bytes(s0_r, s0_rs)
        place(s0_r[...].astype(F32))
        spread()

        @pl.when(s == 1)
        def _():
            go_ahead(0)

    @pl.when(s == 3)
    def _():
        for a, b in PLANE:
            to_p = plane(a, b)
            remote(l3.at[to_p], lc.at[p, :, pl.ds(0, 128)], wa_ss, wa_rs, s, z, to_p).start()
        lc[p, :, 0:128] = l3[p]
        wait_bytes(s0_r, s0_rs)
        yb[0, p] = s0_r[...]
        share_plane(0)

        @pl.loop(0, 8)
        def _(j):
            for i in range(8):
                at = 512 * i + lax.div(p, 4) * 256 + lax.rem(p, 4) * 32 + sub + 128 * half
                hit = (at - ROWS * (8 * z + j) == lane_i) & (lane_i < ROWS)
                lc[j, 32 * i:32 * i + 32, 128:256] = jnp.where(hit, 1.0, 0.0).astype(BF16)

    loads[2].wait()
    q32 = qry_v[...].astype(F32)
    for t in range(32):
        qf[pl.ds(t, 1), :] = q32[0:1, 128 * t:128 * t + 128]
        qf[pl.ds(32 + t, 1), :] = q32[1:2, 128 * t:128 * t + 128]
    qown[...] = qf[pl.ds(0, 64), :].astype(BF16)

    @pl.when(s == 1)
    def _():
        qb[d] = qown[...]


    @pl.when(s == 1)
    def _():
        for dz in OFFSETS[:-1]:
            remote(qown, qb.at[d], qz_ss, qz_rs, s, lax.rem(z + dz, 8), p).start()

    pl.semaphore_wait(line, 7)

    for at_s, to_s in ((0, 3), (2, 0)):
        @pl.when(s == at_s)
        def _():
            for dz in OFFSETS:
                remote(qown, qb.at[d], qz_ss, qz_rs, to_s, lax.rem(z + dz, 8), p).start()

    @pl.when(s == 3)
    def _():
        remote(qown, q3.at[d], qz_ss, q3z_rs, 1, z, p).start()

    @pl.when((s == 1) | (s == 2))
    def _():
        relay()

    @pl.when(s == 2)
    def _():
        yz[z] = summed(0).astype(BF16)
        for dz in OFFSETS[:-1]:
            remote(yz.at[z], yz.at[z], v_ss, v_rs.at[z], s, lax.rem(z + dz, 8), p).start()
        line_product()
        project_inputs()
        remote(x2, xr, x_ss, x_rs, 0, z, p).start()
        for c in loads[6:9]:
            c.wait()

    @pl.when(s == 3)
    def _():
        wait_bytes(l3.at[pl.ds(0, 7)], wa_rs)
        wait_bytes(yb.at[0, pl.ds(0, 7)], y_rs.at[0])
        plane_product(0)
        project_inputs()
        for c in loads[6:9]:
            c.wait()
        projected(top_v, pout_v)
        for n in range(2):
            sk_s[pl.ds(32 * n, 32), :] = sketch(n, x2).astype(BF16)
        remote(sk_s, sk_r, sk_ss, sk_rs, 1, z, p).start()
        wait_bytes(qb.at[pl.ds(0, 8)], qz_rs)
        pass_queries(qb, qp_ss.at[0], qp_rs.at[0], 0, 4)
        yb[1, p] = summed(0).astype(BF16)
        share_plane(1)
        wait_bytes(yb.at[1, pl.ds(0, 7)], y_rs.at[1])
        plane_product(1)
        wait_queries(qb, qp_rs.at[0], 28)
        turn_queries(qb, qg, 0, 4)
        wait_bytes(ar_r, ar_rs)
        total = ar_r[0].astype(F32)
        for i in range(1, 8):
            total = total + ar_r[i].astype(F32)
        yb[2] = total.reshape(8, 32, 128).astype(BF16)
        plane_product(2)
        pass_queries(qb, qp_ss.at[1], qp_rs.at[1], 4, 4)
        gather_line(7)

    def pass_own(blocks):
        wait_bytes(qb.at[pl.ds(0, blocks)], qz_rs)
        for i in range(2):
            pass_queries(qb, qp_ss.at[i], qp_rs.at[i], 4 * i, 4)

    @pl.when(s == 0)
    def _():
        pl.semaphore_wait(gate, 1)

    @pl.when(s == 1)
    def _():
        wait_bytes(q3.at[0], q3z_rs)
        for a, b in PLANE:
            remote(q3.at[d], q3.at[d], q3p_ss, q3p_rs, s, z, plane(a, b)).start()
        pass_own(7)

    @pl.when(s < 2)
    def _():
        project_inputs()
        for c in loads[6:9]:
            c.wait()

    @pl.when(s == 1)
    def _():
        wait_bytes(q3.at[pl.ds(0, 7)], q3p_rs)
        span = q3.at[pl.ds(pl.multiple_of(8 * z, 8), 8)]
        for dz in OFFSETS[:-1]:
            remote(span, span, q3v_ss, q3v_rs, s, lax.rem(z + dz, 8), p).start()

    @pl.when(s == 0)
    def _():
        remote(x2, xr, x_ss, x_rs, 3, z, p).start()

    def turn_own():
        for i in range(2):
            wait_queries(qb, qp_rs.at[i], 28)
            turn_queries(qb, qg, 4 * i, 4)

    @pl.when(s == 1)
    def _():
        turn_own()

    @pl.when(s < 2)
    def _():
        gather_line()

    @pl.when(s == 0)
    def _():
        pass_own(8)

    @pl.when(s != 2)
    def _():
        gather_plane()

        @pl.when(s == 3)
        def _():
            wait_queries(qb, qp_rs.at[1], 28)
            turn_queries(qb, qg, 4, 4)

        @pl.when(s == 1)
        def _():
            wait_queries(q3, q3v_rs)
            turn_queries(q3, qg3)
            xr[...] = x2[...]

        @pl.when(s != 1)
        def _():
            wait_bytes(xr, x_rs)

        project_tokens()
        flat[...] = jnp.zeros((16, R * R), F32)
        for n in range(2):
            lay_flat(n, sketch(n, xr), flat)

        @pl.when(s == 0)
        def _():
            turn_own()

        ex[slot] = scored(qg)

        @pl.when(s == 1)
        def _():
            wait_bytes(sk_r, sk_rs)
            for n in range(2):
                lay_flat(n, sk_r[pl.ds(32 * n, 32), :].astype(F32), flat)
            ex[slot] += scored(qg3)

        for j in (2, 3, 1):
            remote(ex.at[slot], ex.at[slot], ex_ss, ex_rs, lax.rem(s + j, 4), z, p).start()

    @pl.when(s != 2)
    def _():
        wait_bytes(ex.at[pl.ds(0, 2)], ex_rs)

    @pl.when(s == 2)
    def _():
        wait_bytes(ex, ex_rs)
    total = ex[0] + ex[1] + ex[2]
    mine = jnp.zeros((8, 32), F32)
    for i in range(4):
        mine = mine + jnp.where(s == i, total[:, 32 * i:32 * i + 32], 0.0)
    out_ref[...] = mine[0:2, :]

    @pl.when(s < 3)
    def _():
        wait_bytes(s0_s, s0_ss)

    @pl.when(s != 2)
    def _():
        wait_bytes(ex, ex_ss)
        wait_bytes(ag.at[pl.ds(0, 49)], ap_ss)
        for i in range(2):
            wait_bytes(qb.at[pl.ds(0, 28)], qp_ss.at[i])

        @pl.when(z < 7)
        def _():
            wait_bytes(ag.at[pl.ds(0, 7)], az_ss)

    @pl.when(s == 1)
    def _():
        wait_bytes(qb.at[pl.ds(0, 7)], qz_ss)
        wait_bytes(q3.at[pl.ds(0, 7)], q3p_ss)
        wait_bytes(q3.at[pl.ds(0, 56)], q3v_ss)

    @pl.when(s == 3)
    def _():
        wait_bytes(qown, qz_ss)

    @pl.when((s == 0) | (s == 2))
    def _():
        wait_bytes(qb.at[pl.ds(0, 8)], qz_ss)

    @pl.when((s == 0) | (s == 2))
    def _():
        wait_bytes(xr, x_ss)

    @pl.when(s == 3)
    def _():
        wait_bytes(sk_s, sk_ss)

    @pl.when((s == 1) | (s == 2))
    def _():
        wait_bytes(pb, p_ss)
        wait_bytes(zs.at[0], z_ss.at[0])

    @pl.when(s >= 2)
    def _():
        wait_bytes(l3.at[pl.ds(0, 7)], wa_ss)

    @pl.when(s == 2)
    def _():
        wait_bytes(yz.at[pl.ds(0, 7)], v_ss)
        wait_bytes(ar_r, ar_ss)

    @pl.when(s == 3)
    def _():
        for k in range(2):
            wait_bytes(zs.at[k], z_ss.at[k])
        wait_bytes(zs.at[2, pl.ds(0, 7)], z_ss.at[2])
        for k in range(2):
            wait_bytes(yb.at[k, pl.ds(0, 7)], y_ss.at[k])


def local(top_grad, activations, weights, proj_in, proj_out, queries, lengths):
    dma = pltpu.SemaphoreType.DMA
    anywhere = pl.BlockSpec(memory_space=pl.ANY)
    return pl.pallas_call(
        kernel,
        out_shape=jax.ShapeDtypeStruct((2, 32), F32),
        in_specs=[anywhere] * 6 + [pl.BlockSpec(memory_space=pltpu.SMEM)],
        out_specs=pl.BlockSpec(memory_space=pltpu.VMEM),
        scratch_shapes=[
            pltpu.VMEM((ROWS, D), BF16),
            pltpu.VMEM((R, 256), BF16),
            pltpu.VMEM((2, R * R), BF16),
            pltpu.VMEM((2 * R, D), BF16),
            pltpu.VMEM((2 * R, D), BF16),
            pltpu.VMEM((TOK, D), BF16),
            pltpu.VMEM((TOK, D), BF16),
            pltpu.VMEM((D + 16, 128), F32),
            pltpu.VMEM((2048, 256), BF16),
            pltpu.VMEM((8, 256, 128), BF16),
            pltpu.VMEM((8, 256, 128), BF16),
            pltpu.VMEM((8, 256, 256), BF16),
            pltpu.VMEM((256, 128), BF16),
            pltpu.VMEM((8, 128, 128), BF16),
            pltpu.VMEM((8, 256, 128), BF16),
            pltpu.VMEM((32, 128), BF16),
            pltpu.VMEM((32, 128), BF16),
            pltpu.VMEM((8, 8, 32, 128), BF16),
            pltpu.VMEM((7, 8, 32, 128), BF16),
            pltpu.VMEM((8, 32, 128), BF16),
            pltpu.VMEM((3, 8, 32, 128), BF16),
            pltpu.VMEM((8, 32, 128), F32),
            pltpu.VMEM((TOK, 128), BF16),
            pltpu.VMEM((8, TOK, 128), BF16),
            pltpu.VMEM((3, 8, 32, 128), BF16),
            pltpu.VMEM((2, 8, 32, 128), BF16),
            pltpu.VMEM((64, 32, 128), BF16),
            pltpu.VMEM((64, 128), BF16),
            pltpu.VMEM((64, 64, 128), BF16),
            pltpu.VMEM((64, 64, 128), BF16),
            pltpu.VMEM((4096, 128), F32),
            pltpu.VMEM((R * R, 128), BF16),
            pltpu.VMEM((R * R, 128), BF16),
            pltpu.VMEM((TOK, 128), F32),
            pltpu.VMEM((TOK, 128), BF16),
            pltpu.VMEM((TOK, 128), BF16),
            pltpu.VMEM((128, 128), F32),
            pltpu.VMEM((64, 128), BF16),
            pltpu.VMEM((64, 128), BF16),
            pltpu.VMEM((16, R * R), F32),
            pltpu.VMEM((3, 8, 128), F32),
            dma((9,)),
            dma, dma,
            dma, dma((4,)),
            dma((3,)), dma((2,)),
            dma, dma((8,)),
            dma, dma((8,)),
            dma, dma, dma((2,)), dma((2,)),
            dma, dma, dma, dma((8,)), dma((2,)), dma((2,)), dma, dma,
            dma, dma, dma, dma, dma, dma, dma, dma, dma,
            dma, dma,
            pltpu.SemaphoreType.REGULAR,
            pltpu.SemaphoreType.REGULAR,
        ],
        compiler_params=pltpu.CompilerParams(
            collective_id=0, has_side_effects=True, vmem_limit_bytes=64 * 2**20 - 2**17
        ),
        name="chain",
    )(top_grad, activations, weights, proj_in, proj_out, queries, lengths) * 0.125


def solution(mesh):
    in_specs = (
        P("dp", None),
        P("section", "dp", None),
        P("section", "dp", None),
        P("section", None, None),
        P("section", None, None),
        P("section", "dp", None),
        P("dp"),
    )
    return jax.shard_map(local, mesh=mesh, in_specs=in_specs, out_specs=P("dp", "section"), check_vma=False)
```

```python
import functools

import jax
import jax.numpy as jnp
from jax import lax
from jax.experimental import pallas as pl
from jax.experimental.pallas import tpu as pltpu
from jax.sharding import PartitionSpec as P

D = 3584
R = 64
ROWS = 56
SEQ = 128
TOK = 256
MESH = pl.DeviceIdType.MESH
F32 = jnp.float32
BF16 = jnp.bfloat16
OFFSETS = (4, 3, 5, 2, 6, 1, 7, 0)
PARTS = ((0, 1), (1, 3), (3, 5), (5, 8))
PLANE = tuple((a, b) for a in (2, 1, 3, 0) for b in (1, 0) if a or b)


def nt(a, b):
    return lax.dot_general(a, b, (((1,), (1,)), ((), ())), preferred_element_type=F32)


def kernel(
    top_ref, act_ref, w_ref, pin_ref, pout_ref, qry_ref, len_ref, out_ref,
    w_v, win_v, qry_v, pin_v, pout_v, act_v, top_v,
    wt, le, l3, lb, lc, rr, s0_s, s0_r, ob, pb, yz, yb, bs, ar_s, ar_r, zs, zb, ag, qown, qb, q3, qf, qg, qg3, acc, x2, xr, skf, sk_s, sk_r, flat, ex,
    ld, s0_ss, s0_rs, p_ss, p_rs, z_ss, z_rs, az_ss, az_rs, ap_ss, ap_rs, qz_ss, qz_rs, qp_ss, qp_rs,
    wa_ss, wa_rs, v_ss, v_rs, y_ss, y_rs, ar_ss, ar_rs, q3z_rs, q3p_ss, q3p_rs, q3v_ss, q3v_rs, x_ss, x_rs, sk_ss, sk_rs, ex_ss, ex_rs, gate, line,
):
    s = lax.axis_index("section")
    d = lax.axis_index("dp")
    z = lax.div(d, 8)
    p = lax.rem(d, 8)
    y = lax.div(p, 2)
    x = lax.rem(p, 2)
    lane = lax.broadcasted_iota(jnp.int32, (32, 128), 1)
    low = lane < 64

    def plane(a, b):
        return 2 * lax.rem(y + a, 4) + lax.rem(x + b, 2)

    def remote(src, dst, ss, rs, section, at_z, at_p):
        return pltpu.make_async_remote_copy(
            src_ref=src, dst_ref=dst, send_sem=ss, recv_sem=rs,
            device_id=(section, at_z * 8 + at_p), device_id_type=MESH,
        )

    def wait_bytes(ref, sem):
        pltpu.make_async_copy(ref, ref, sem).wait()

    bar = pltpu.get_barrier_semaphore()
    for dz in OFFSETS[:-1]:
        pl.semaphore_signal(bar, inc=1, device_id=(s, lax.rem(z + dz, 8) * 8 + p), device_id_type=MESH)
    for ds in (2, 3, 1):
        pl.semaphore_signal(bar, inc=1, device_id=(lax.rem(s + ds, 4), d), device_id_type=MESH)
    for a, b in PLANE:
        pl.semaphore_signal(bar, inc=1, device_id=(s, z * 8 + plane(a, b)), device_id_type=MESH)

    tile = jnp.minimum(lax.div(ROWS * d, 128), D // 128 - 2)
    loads = [
        pltpu.make_async_copy(pout_ref.at[0, :, pl.ds(pl.multiple_of(tile * 128, 128), 256)], win_v, ld.at[0]),
        pltpu.make_async_copy(w_ref.at[0], w_v, ld.at[1]),
        pltpu.make_async_copy(qry_ref.at[0], qry_v, ld.at[2]),
        pltpu.make_async_copy(act_ref.at[0], act_v, ld.at[3]),
        pltpu.make_async_copy(pin_ref.at[0], pin_v.at[pl.ds(0, R)], ld.at[4]),
        pltpu.make_async_copy(pin_ref.at[0], pin_v.at[pl.ds(R, R)], ld.at[5]),
        pltpu.make_async_copy(top_ref, top_v, ld.at[6]),
        pltpu.make_async_copy(pout_ref.at[0], pout_v.at[pl.ds(0, R)], ld.at[7]),
        pltpu.make_async_copy(pout_ref.at[0], pout_v.at[pl.ds(R, R)], ld.at[8]),
    ]
    for c in loads:
        c.start()

    ag[pl.ds(56, 8)] = jnp.zeros((8, 32, 128), BF16)

    lane_i = jnp.bitwise_and(lane, 63)
    half = jnp.right_shift(lane, 6)
    sub = lax.broadcasted_iota(jnp.int32, (32, 128), 0)

    @pl.when((s == 1) | (s == 2))
    def _():
        le[:, pl.ds(128, 128)] = jnp.zeros((2048, 128), BF16)
        hit = (sub + 32 * half == lane_i) & (lane_i < ROWS)
        le[pl.ds(pl.multiple_of(d * 32, 32), 32), pl.ds(128, 128)] = jnp.where(hit, 1.0, 0.0).astype(BF16)

    loads[0].wait()
    first = ROWS * d - 128 * tile
    row = lax.broadcasted_iota(jnp.int32, (32, 256), 0)
    col = lax.broadcasted_iota(jnp.int32, (32, 256), 1) - first
    pick_low = jnp.where(col == row, 1.0, 0.0).astype(BF16)
    pick_high = jnp.where((col == row + 32) & (row < ROWS - 32), 1.0, 0.0).astype(BF16)
    window = win_v[...]
    both = jnp.concatenate([window, window], axis=0)
    s0_s[...] = jnp.where(low, nt(pick_low, both), nt(pick_high, both)).astype(BF16)

    loads[1].wait()

    @pl.when(s >= 1)
    def _():
        @pl.loop(0, D // 128, unroll=7)
        def _(c):
            part = w_v[:, pl.ds(pl.multiple_of(c * 128, 128), 128)].astype(F32)
            gap = jnp.zeros((R - ROWS, 128), F32)
            wt[pl.ds(pl.multiple_of(c * 128, 128), 128), :] = jnp.concatenate([part, gap, part, gap], axis=0).T

        wt[pl.ds(D, 16), :] = jnp.zeros((16, 128), F32)

        @pl.when(s < 3)
        def _():
            @pl.loop(0, 64, unroll=8)
            def _(c):
                one = wt[pl.ds(pl.multiple_of(c * ROWS, 8), 32), :]
                two = wt[pl.ds(pl.multiple_of(c * ROWS + 32, 8), 32), :]
                le[pl.ds(pl.multiple_of(c * 32, 32), 32), pl.ds(0, 128)] = jnp.where(low, one, two).astype(BF16)

        @pl.when(s == 3)
        def _():
            @pl.loop(0, 7)
            def _(i):
                for j in range(8):
                    at = 512 * i + 256 * (j // 4) + 32 * (j % 4)
                    one = wt[pl.ds(pl.multiple_of(at, 32), 32), :]
                    two = wt[pl.ds(pl.multiple_of(at + 128, 32), 32), :]
                    l3[j, pl.ds(pl.multiple_of(i * 32, 32), 32), :] = jnp.where(low, one, two).astype(BF16)

            l3[:, pl.ds(224, 32), :] = jnp.zeros((8, 32, 128), BF16)

    pl.semaphore_wait(bar, 17)

    @pl.when(s < 3)
    def _():
        remote(s0_s, s0_r, s0_ss, s0_rs, s + 1, z, p).start()

    for dz in OFFSETS[:-1]:
        pl.semaphore_signal(line, inc=1, device_id=(s, lax.rem(z + dz, 8) * 8 + p), device_id_type=MESH)

    def turned_parts(packed):
        turned = pltpu.roll(packed, 64, 1)
        zero = jnp.zeros((32, 128), F32)
        return [
            part.astype(BF16) for part in (
                jnp.where(low, packed, zero), jnp.where(low, turned, zero),
                jnp.where(low, zero, turned), jnp.where(low, zero, packed),
            )
        ]

    def place(packed):
        for i, part in enumerate(turned_parts(packed)):
            rr[pl.ds(32 * i, 32), :] = part
            rr[pl.ds(128 + 32 * i, 32), :] = part

    def summed(slot, count=8):
        wait_bytes(zb.at[slot, pl.ds(0, count)], z_rs.at[slot])
        total = zb[slot, 0].astype(F32)
        for i in range(1, 8):
            total = total + zb[slot, i].astype(F32)
        return total

    def spread():
        for part, (lo, hi) in enumerate(PARTS):
            for i in range(lo, hi):
                at = pl.ds(pl.multiple_of(lax.rem(z + OFFSETS[i], 8) * 256, 256), 256)
                ob[:, i] = jnp.dot(le[at, :], rr[...], preferred_element_type=F32).astype(BF16).reshape(8, 32, 128)
            for j, (a, b) in enumerate(PLANE):
                to_p = plane(a, b)
                span = pl.ds(lo, hi - lo)
                remote(ob.at[to_p, span], pb.at[j, span], p_ss, p_rs.at[part], s, z, to_p).start()

    def relay():
        for part, (lo, hi) in enumerate(PARTS):
            wait_bytes(pb.at[pl.ds(0, hi - lo), pl.ds(0, 7)], p_rs.at[part])
            for i in range(lo, hi):
                total = ob[p, i].astype(F32)
                for j in range(7):
                    total = total + pb[j, i].astype(F32)
                zs[0, i] = total.astype(BF16)
                to_z = lax.rem(z + OFFSETS[i], 8)
                remote(zs.at[0, i], zb.at[0, z], z_ss.at[0], z_rs.at[0], s + 1, to_z, p).start()

    def send_columns():
        for dz in OFFSETS[:-1]:
            to_z = lax.rem(z + dz, 8)
            block = le.at[pl.ds(pl.multiple_of(to_z * 256, 256), 256), pl.ds(0, 128)]
            remote(block, lb.at[z], wa_ss, wa_rs, s, to_z, p).start()
        lb[z] = le[pl.ds(pl.multiple_of(z * 256, 256), 256), pl.ds(0, 128)]

    def line_product():
        wait_bytes(l3.at[pl.ds(0, 7)], wa_rs)
        total = jnp.zeros((TOK, 128), F32)
        for dz in nearest:
            from_z = lax.rem(z + dz, 8)
            if dz:
                wait_bytes(yz.at[from_z], v_rs.at[from_z])
            right = jnp.concatenate(turned_parts(yz[from_z].astype(F32)), axis=0)
            total = total + jnp.dot(lb[from_z], right, preferred_element_type=F32)
        bs[...] = total.reshape(8, 32, 128)
        bs[p] += yz[z].astype(F32)
        ar_s[...] = bs[...].reshape(TOK, 128).astype(BF16)
        for a, b in PLANE + ((0, 0),):
            remote(ar_s, ar_r.at[p], ar_ss, ar_rs, 3, z, plane(a, b)).start()

    def plane_product(k):
        total = jnp.zeros((TOK, 128), F32)
        for j in range(8):
            parts = turned_parts(yb[k, j].astype(F32))
            total = total + jnp.dot(lc[j], jnp.concatenate(parts + parts, axis=0), preferred_element_type=F32)
        zs[k] = total.astype(BF16).reshape(8, 32, 128)
        for dz in OFFSETS:
            to_z = lax.rem(z + dz, 8)
            if k == 2 and dz == 0:
                zb[1, z] = zs[k, z]
            else:
                remote(zs.at[k, to_z], zb.at[1, z], z_ss.at[k], z_rs.at[1], (0, 1, 3)[k], to_z, p).start()

    def share_plane(k):
        for a, b in PLANE:
            remote(yb.at[k, p], yb.at[k, p], y_ss.at[k], y_rs.at[k], s, z, plane(a, b)).start()

    def projected(tokens, both_proj):
        acc[...] = jnp.zeros((TOK, 128), F32)

        @pl.loop(0, 7)
        def _(c):
            at = pl.ds(pl.multiple_of(c * 512, 512), 512)
            acc[...] += nt(tokens[:, at], both_proj[:, at])

    def pass_queries(held, ss, rs, first=0, count=8):
        for a, b in PLANE:
            to_p = plane(a, b)

            @pl.loop(first, first + count)
            def _(i):
                block = held.at[i * 8 + p]
                remote(block, block, ss, rs, s, z, to_p).start()

    def turn_queries(held, turned, first=0, count=8):
        @pl.loop(8 * first, 8 * (first + count))
        def _(c):
            qf[pl.ds(pl.multiple_of(c * 64, 64), 64), :] = held[c].astype(F32)

        for t in range(32):
            rows = qf[pl.ds(512 * first + t, 16 * count, stride=32), :]
            turned[128 * t:128 * t + 128, 16 * first:16 * (first + count)] = rows.T.astype(BF16)

    def scored(turned):
        return jnp.dot(flat[...].astype(BF16), turned[...], preferred_element_type=F32)[0:8]

    def wait_queries(held, rs, blocks=56):
        wait_bytes(held.at[pl.ds(0, blocks)], rs)

    def go_ahead(to_s):
        pl.semaphore_signal(gate, inc=1, device_id=(to_s, d), device_id_type=MESH)

    def project_inputs():
        for c in loads[3:6]:
            c.wait()
        projected(act_v, pin_v)
        x2[...] = acc[...].astype(BF16)

    position = lax.broadcasted_iota(jnp.int32, (SEQ, 128), 0)

    def sketch(n, held):
        length = len_ref[n]
        rows = pl.ds(n * SEQ, SEQ)
        g = jnp.where(position < length, acc[rows, :], 0.0).astype(BF16)
        skf[...] = lax.dot_general(g, held[rows, :], (((0,), (0,)), ((), ())), preferred_element_type=F32)
        pairs = jnp.where(low, skf[pl.ds(0, 32, stride=2), :], skf[pl.ds(1, 32, stride=2), :])
        return pairs / jnp.full((32, 128), length, jnp.int32).astype(F32)

    def lay_flat(n, pairs, to):
        for t in range(32):
            to[pl.ds(n, 1), 128 * t:128 * t + 128] = pairs[t:t + 1, :]

    slot = jnp.minimum(s, 2)
    nearest = (0, 1, 7, 2, 6, 3, 5, 4)

    def gather_line(count=8):
        total = summed(1, count).astype(BF16)

        @pl.when(z < 7)
        def _():
            ag[d] = total
            for dz in OFFSETS[:-1]:
                remote(ag.at[d], ag.at[d], az_ss, az_rs.at[z], s, lax.rem(z + dz, 8), p).start()

    def gather_plane():
        for dz in nearest:
            from_z = lax.rem(z + dz, 8)

            @pl.when(from_z < 7)
            def _():
                block = ag.at[from_z * 8 + p]
                if dz:
                    wait_bytes(block, az_rs.at[from_z])
                for a, b in PLANE:
                    remote(block, block, ap_ss, ap_rs.at[from_z], s, z, plane(a, b)).start()

    def project_tokens():
        wide = lax.broadcasted_iota(jnp.int32, (128, 128), 1) < 64
        acc[...] = jnp.zeros((TOK, 128), F32)
        for group in ((0, 1, 7), (2, 6), (3, 5), (4,)):
            for dz in group:
                from_z = lax.rem(z + dz, 8)

                @pl.when(from_z < 7)
                def _():
                    wait_bytes(ag.at[pl.ds(0, 7)], ap_rs.at[from_z])

            total = acc[...]
            for dz in group:
                from_z = lax.rem(z + dz, 8)
                parts = []
                for c in range(2):
                    piece = ag[pl.ds(from_z * 8 + 4 * c, 4)].reshape(128, 128)
                    zero = jnp.zeros_like(piece)
                    parts += [jnp.where(wide, piece, zero), jnp.where(wide, zero, piece)]
                at = pl.ds(pl.multiple_of(lax.rem(from_z, 7) * 512, 512), 512)
                total = total + jnp.dot(top_v[:, at], jnp.concatenate(parts, axis=0), preferred_element_type=F32)
            acc[...] = total
        acc[...] = acc[...] + pltpu.roll(acc[...], 64, 1)

    @pl.when(s == 2)
    def _():
        send_columns()

    @pl.when((s == 1) | (s == 2))
    def _():
        wait_bytes(s0_r, s0_rs)
        place(s0_r[...].astype(F32))
        spread()

        @pl.when(s == 1)
        def _():
            go_ahead(0)

    @pl.when(s == 3)
    def _():
        for a, b in PLANE:
            to_p = plane(a, b)
            remote(l3.at[to_p], lc.at[p, :, pl.ds(0, 128)], wa_ss, wa_rs, s, z, to_p).start()
        lc[p, :, 0:128] = l3[p]
        wait_bytes(s0_r, s0_rs)
        yb[0, p] = s0_r[...]
        share_plane(0)

        @pl.loop(0, 8)
        def _(j):
            for i in range(8):
                at = 512 * i + lax.div(p, 4) * 256 + lax.rem(p, 4) * 32 + sub + 128 * half
                hit = (at - ROWS * (8 * z + j) == lane_i) & (lane_i < ROWS)
                lc[j, 32 * i:32 * i + 32, 128:256] = jnp.where(hit, 1.0, 0.0).astype(BF16)

    loads[2].wait()
    q32 = qry_v[...].astype(F32)
    for t in range(32):
        qf[pl.ds(t, 1), :] = q32[0:1, 128 * t:128 * t + 128]
        qf[pl.ds(32 + t, 1), :] = q32[1:2, 128 * t:128 * t + 128]
    qown[...] = qf[pl.ds(0, 64), :].astype(BF16)

    @pl.when(s == 1)
    def _():
        qb[d] = qown[...]


    @pl.when(s == 1)
    def _():
        for dz in OFFSETS[:-1]:
            remote(qown, qb.at[d], qz_ss, qz_rs, s, lax.rem(z + dz, 8), p).start()

    pl.semaphore_wait(line, 7)

    for at_s, to_s in ((0, 3), (2, 0)):
        @pl.when(s == at_s)
        def _():
            for dz in OFFSETS:
                remote(qown, qb.at[d], qz_ss, qz_rs, to_s, lax.rem(z + dz, 8), p).start()

    @pl.when(s == 3)
    def _():
        remote(qown, q3.at[d], qz_ss, q3z_rs, 1, z, p).start()

    @pl.when((s == 1) | (s == 2))
    def _():
        relay()

    @pl.when(s == 2)
    def _():
        yz[z] = summed(0).astype(BF16)
        for dz in OFFSETS[:-1]:
            remote(yz.at[z], yz.at[z], v_ss, v_rs.at[z], s, lax.rem(z + dz, 8), p).start()
        line_product()
        project_inputs()
        remote(x2, xr, x_ss, x_rs, 0, z, p).start()
        for c in loads[6:9]:
            c.wait()

    @pl.when(s == 3)
    def _():
        wait_bytes(l3.at[pl.ds(0, 7)], wa_rs)
        wait_bytes(yb.at[0, pl.ds(0, 7)], y_rs.at[0])
        plane_product(0)
        project_inputs()
        for c in loads[6:9]:
            c.wait()
        projected(top_v, pout_v)
        for n in range(2):
            sk_s[pl.ds(32 * n, 32), :] = sketch(n, x2).astype(BF16)
        remote(sk_s, sk_r, sk_ss, sk_rs, 1, z, p).start()
        wait_bytes(qb.at[pl.ds(0, 8)], qz_rs)
        pass_queries(qb, qp_ss.at[0], qp_rs.at[0], 0, 4)
        yb[1, p] = summed(0).astype(BF16)
        share_plane(1)
        wait_bytes(yb.at[1, pl.ds(0, 7)], y_rs.at[1])
        plane_product(1)
        wait_queries(qb, qp_rs.at[0], 28)
        turn_queries(qb, qg, 0, 4)
        wait_bytes(ar_r, ar_rs)
        total = ar_r[0].astype(F32)
        for i in range(1, 8):
            total = total + ar_r[i].astype(F32)
        yb[2] = total.reshape(8, 32, 128).astype(BF16)
        plane_product(2)
        pass_queries(qb, qp_ss.at[1], qp_rs.at[1], 4, 4)
        gather_line(7)

    def pass_own(blocks):
        wait_bytes(qb.at[pl.ds(0, blocks)], qz_rs)
        for i in range(2):
            pass_queries(qb, qp_ss.at[i], qp_rs.at[i], 4 * i, 4)

    @pl.when(s == 0)
    def _():
        pl.semaphore_wait(gate, 1)

    @pl.when(s == 1)
    def _():
        wait_bytes(q3.at[0], q3z_rs)
        for a, b in PLANE:
            remote(q3.at[d], q3.at[d], q3p_ss, q3p_rs, s, z, plane(a, b)).start()
        pass_own(7)

    @pl.when(s < 2)
    def _():
        project_inputs()
        for c in loads[6:9]:
            c.wait()

    @pl.when(s == 1)
    def _():
        wait_bytes(q3.at[pl.ds(0, 7)], q3p_rs)
        span = q3.at[pl.ds(pl.multiple_of(8 * z, 8), 8)]
        for dz in OFFSETS[:-1]:
            remote(span, span, q3v_ss, q3v_rs, s, lax.rem(z + dz, 8), p).start()

    @pl.when(s == 0)
    def _():
        remote(x2, xr, x_ss, x_rs, 3, z, p).start()

    def turn_own():
        for i in range(2):
            wait_queries(qb, qp_rs.at[i], 28)
            turn_queries(qb, qg, 4 * i, 4)

    @pl.when(s == 1)
    def _():
        turn_own()

    @pl.when(s < 2)
    def _():
        gather_line()

    @pl.when(s == 0)
    def _():
        pass_own(8)

    @pl.when(s != 2)
    def _():
        gather_plane()

        @pl.when(s == 3)
        def _():
            wait_queries(qb, qp_rs.at[1], 28)
            turn_queries(qb, qg, 4, 4)

        @pl.when(s == 1)
        def _():
            wait_queries(q3, q3v_rs)
            turn_queries(q3, qg3)
            xr[...] = x2[...]

        @pl.when(s != 1)
        def _():
            wait_bytes(xr, x_rs)

        project_tokens()
        flat[...] = jnp.zeros((16, R * R), F32)
        for n in range(2):
            lay_flat(n, sketch(n, xr), flat)

        @pl.when(s == 0)
        def _():
            turn_own()

        ex[slot] = scored(qg)

        @pl.when(s == 1)
        def _():
            wait_bytes(sk_r, sk_rs)
            for n in range(2):
                lay_flat(n, sk_r[pl.ds(32 * n, 32), :].astype(F32), flat)
            ex[slot] += scored(qg3)

        for j in (2, 3, 1):
            remote(ex.at[slot], ex.at[slot], ex_ss, ex_rs, lax.rem(s + j, 4), z, p).start()

    @pl.when(s < 3)
    def _():
        wait_bytes(s0_s, s0_ss)

    @pl.when(s != 2)
    def _():
        wait_bytes(ag.at[pl.ds(0, 49)], ap_ss)
        for i in range(2):
            wait_bytes(qb.at[pl.ds(0, 28)], qp_ss.at[i])

        @pl.when(z < 7)
        def _():
            wait_bytes(ag.at[pl.ds(0, 7)], az_ss)

    @pl.when(s == 1)
    def _():
        wait_bytes(qb.at[pl.ds(0, 7)], qz_ss)
        wait_bytes(q3.at[pl.ds(0, 7)], q3p_ss)
        wait_bytes(q3.at[pl.ds(0, 56)], q3v_ss)

    @pl.when(s == 3)
    def _():
        wait_bytes(qown, qz_ss)

    @pl.when((s == 0) | (s == 2))
    def _():
        wait_bytes(qb.at[pl.ds(0, 8)], qz_ss)

    @pl.when((s == 0) | (s == 2))
    def _():
        wait_bytes(xr, x_ss)

    @pl.when(s == 3)
    def _():
        wait_bytes(sk_s, sk_ss)

    @pl.when((s == 1) | (s == 2))
    def _():
        wait_bytes(pb, p_ss)
        wait_bytes(zs.at[0], z_ss.at[0])

    @pl.when(s >= 2)
    def _():
        wait_bytes(l3.at[pl.ds(0, 7)], wa_ss)

    @pl.when(s == 2)
    def _():
        wait_bytes(yz.at[pl.ds(0, 7)], v_ss)
        wait_bytes(ar_r, ar_ss)

    @pl.when(s == 3)
    def _():
        for k in range(2):
            wait_bytes(zs.at[k], z_ss.at[k])
        wait_bytes(zs.at[2, pl.ds(0, 7)], z_ss.at[2])
        for k in range(2):
            wait_bytes(yb.at[k, pl.ds(0, 7)], y_ss.at[k])

    @pl.when(s != 2)
    def _():
        wait_bytes(ex.at[pl.ds(0, 2)], ex_rs)

    @pl.when(s == 2)
    def _():
        wait_bytes(ex, ex_rs)
    total = ex[0] + ex[1] + ex[2]
    mine = jnp.zeros((8, 32), F32)
    for i in range(4):
        mine = mine + jnp.where(s == i, total[:, 32 * i:32 * i + 32], 0.0)
    out_ref[...] = mine[0:2, :]

    @pl.when(s != 2)
    def _():
        wait_bytes(ex, ex_ss)


def local(top_grad, activations, weights, proj_in, proj_out, queries, lengths):
    dma = pltpu.SemaphoreType.DMA
    anywhere = pl.BlockSpec(memory_space=pl.ANY)
    return pl.pallas_call(
        kernel,
        out_shape=jax.ShapeDtypeStruct((2, 32), F32),
        in_specs=[anywhere] * 6 + [pl.BlockSpec(memory_space=pltpu.SMEM)],
        out_specs=pl.BlockSpec(memory_space=pltpu.VMEM),
        scratch_shapes=[
            pltpu.VMEM((ROWS, D), BF16),
            pltpu.VMEM((R, 256), BF16),
            pltpu.VMEM((2, R * R), BF16),
            pltpu.VMEM((2 * R, D), BF16),
            pltpu.VMEM((2 * R, D), BF16),
            pltpu.VMEM((TOK, D), BF16),
            pltpu.VMEM((TOK, D), BF16),
            pltpu.VMEM((D + 16, 128), F32),
            pltpu.VMEM((2048, 256), BF16),
            pltpu.VMEM((8, 256, 128), BF16),
            pltpu.VMEM((8, 256, 128), BF16),
            pltpu.VMEM((8, 256, 256), BF16),
            pltpu.VMEM((256, 128), BF16),
            pltpu.VMEM((32, 128), BF16),
            pltpu.VMEM((32, 128), BF16),
            pltpu.VMEM((8, 8, 32, 128), BF16),
            pltpu.VMEM((7, 8, 32, 128), BF16),
            pltpu.VMEM((8, 32, 128), BF16),
            pltpu.VMEM((3, 8, 32, 128), BF16),
            pltpu.VMEM((8, 32, 128), F32),
            pltpu.VMEM((TOK, 128), BF16),
            pltpu.VMEM((8, TOK, 128), BF16),
            pltpu.VMEM((3, 8, 32, 128), BF16),
            pltpu.VMEM((2, 8, 32, 128), BF16),
            pltpu.VMEM((64, 32, 128), BF16),
            pltpu.VMEM((64, 128), BF16),
            pltpu.VMEM((64, 64, 128), BF16),
            pltpu.VMEM((64, 64, 128), BF16),
            pltpu.VMEM((4096, 128), F32),
            pltpu.VMEM((R * R, 128), BF16),
            pltpu.VMEM((R * R, 128), BF16),
            pltpu.VMEM((TOK, 128), F32),
            pltpu.VMEM((TOK, 128), BF16),
            pltpu.VMEM((TOK, 128), BF16),
            pltpu.VMEM((128, 128), F32),
            pltpu.VMEM((64, 128), BF16),
            pltpu.VMEM((64, 128), BF16),
            pltpu.VMEM((16, R * R), F32),
            pltpu.VMEM((3, 8, 128), F32),
            dma((9,)),
            dma, dma,
            dma, dma((4,)),
            dma((3,)), dma((2,)),
            dma, dma((8,)),
            dma, dma((8,)),
            dma, dma, dma((2,)), dma((2,)),
            dma, dma, dma, dma((8,)), dma((2,)), dma((2,)), dma, dma,
            dma, dma, dma, dma, dma, dma, dma, dma, dma,
            dma, dma,
            pltpu.SemaphoreType.REGULAR,
            pltpu.SemaphoreType.REGULAR,
        ],
        compiler_params=pltpu.CompilerParams(
            collective_id=0, has_side_effects=True, vmem_limit_bytes=56541184
        ),
        name="chain",
    )(top_grad, activations, weights, proj_in, proj_out, queries, lengths) * 0.125


def solution(mesh):
    in_specs = (
        P("dp", None),
        P("section", "dp", None),
        P("section", "dp", None),
        P("section", None, None),
        P("section", None, None),
        P("section", "dp", None),
        P("dp"),
    )
    return jax.shard_map(local, mesh=mesh, in_specs=in_specs, out_specs=P("dp", "section"), check_vma=False)
```

```python
import functools

import jax
import jax.numpy as jnp
from jax import lax
from jax.experimental import pallas as pl
from jax.experimental.pallas import tpu as pltpu
from jax.sharding import PartitionSpec as P

D = 3584
R = 64
ROWS = 56
SEQ = 128
TOK = 256
MESH = pl.DeviceIdType.MESH
F32 = jnp.float32
BF16 = jnp.bfloat16
OFFSETS = (4, 3, 5, 2, 6, 1, 7, 0)
PARTS = ((0, 1), (1, 3), (3, 5), (5, 8))
PLANE = tuple((a, b) for a in (2, 1, 3, 0) for b in (1, 0) if a or b)


def nt(a, b):
    return lax.dot_general(a, b, (((1,), (1,)), ((), ())), preferred_element_type=F32)


def kernel(
    top_ref, act_ref, w_ref, pin_ref, pout_ref, qry_ref, len_ref, out_ref,
    w_v, win_v, qry_v, pin_v, pout_v, act_v, top_v,
    wt, le, l3, lb, lc, rr, s0_s, s0_r, ob, pb, yz, yb, bs, ar_s, ar_r, zs, zb, ag, qown, qb, q3, qf, qg, qg3, acc, x2, xr, skf, sk_s, sk_r, flat, ex,
    ld, s0_ss, s0_rs, p_ss, p_rs, z_ss, z_rs, az_ss, az_rs, ap_ss, ap_rs, qz_ss, qz_rs, qp_ss, qp_rs,
    wa_ss, wa_rs, v_ss, v_rs, y_ss, y_rs, ar_ss, ar_rs, q3z_rs, q3p_ss, q3p_rs, q3v_ss, q3v_rs, x_ss, x_rs, sk_ss, sk_rs, ex_ss, ex_rs, gate, line,
):
    s = lax.axis_index("section")
    d = lax.axis_index("dp")
    z = lax.div(d, 8)
    p = lax.rem(d, 8)
    y = lax.div(p, 2)
    x = lax.rem(p, 2)
    lane = lax.broadcasted_iota(jnp.int32, (32, 128), 1)
    low = lane < 64

    def plane(a, b):
        return 2 * lax.rem(y + a, 4) + lax.rem(x + b, 2)

    def remote(src, dst, ss, rs, section, at_z, at_p):
        return pltpu.make_async_remote_copy(
            src_ref=src, dst_ref=dst, send_sem=ss, recv_sem=rs,
            device_id=(section, at_z * 8 + at_p), device_id_type=MESH,
        )

    def wait_bytes(ref, sem):
        pltpu.make_async_copy(ref, ref, sem).wait()

    bar = pltpu.get_barrier_semaphore()
    for dz in OFFSETS[:-1]:
        pl.semaphore_signal(bar, inc=1, device_id=(s, lax.rem(z + dz, 8) * 8 + p), device_id_type=MESH)
    for ds in (2, 3, 1):
        pl.semaphore_signal(bar, inc=1, device_id=(lax.rem(s + ds, 4), d), device_id_type=MESH)
    for a, b in PLANE:
        pl.semaphore_signal(bar, inc=1, device_id=(s, z * 8 + plane(a, b)), device_id_type=MESH)

    tile = jnp.minimum(lax.div(ROWS * d, 128), D // 128 - 2)
    loads = [
        pltpu.make_async_copy(pout_ref.at[0, :, pl.ds(pl.multiple_of(tile * 128, 128), 256)], win_v, ld.at[0]),
        pltpu.make_async_copy(w_ref.at[0], w_v, ld.at[1]),
        pltpu.make_async_copy(qry_ref.at[0], qry_v, ld.at[2]),
        pltpu.make_async_copy(act_ref.at[0], act_v, ld.at[3]),
        pltpu.make_async_copy(pin_ref.at[0], pin_v.at[pl.ds(0, R)], ld.at[4]),
        pltpu.make_async_copy(pin_ref.at[0], pin_v.at[pl.ds(R, R)], ld.at[5]),
        pltpu.make_async_copy(top_ref, top_v, ld.at[6]),
        pltpu.make_async_copy(pout_ref.at[0], pout_v.at[pl.ds(0, R)], ld.at[7]),
        pltpu.make_async_copy(pout_ref.at[0], pout_v.at[pl.ds(R, R)], ld.at[8]),
    ]
    for c in loads:
        c.start()

    ag[pl.ds(56, 8)] = jnp.zeros((8, 32, 128), BF16)

    lane_i = jnp.bitwise_and(lane, 63)
    half = jnp.right_shift(lane, 6)
    sub = lax.broadcasted_iota(jnp.int32, (32, 128), 0)

    @pl.when((s == 1) | (s == 2))
    def _():
        le[:, pl.ds(128, 128)] = jnp.zeros((2048, 128), BF16)
        hit = (sub + 32 * half == lane_i) & (lane_i < ROWS)
        le[pl.ds(pl.multiple_of(d * 32, 32), 32), pl.ds(128, 128)] = jnp.where(hit, 1.0, 0.0).astype(BF16)

    loads[0].wait()
    first = ROWS * d - 128 * tile
    row = lax.broadcasted_iota(jnp.int32, (32, 256), 0)
    col = lax.broadcasted_iota(jnp.int32, (32, 256), 1) - first
    pick_low = jnp.where(col == row, 1.0, 0.0).astype(BF16)
    pick_high = jnp.where((col == row + 32) & (row < ROWS - 32), 1.0, 0.0).astype(BF16)
    window = win_v[...]
    both = jnp.concatenate([window, window], axis=0)
    s0_s[...] = jnp.where(low, nt(pick_low, both), nt(pick_high, both)).astype(BF16)

    loads[1].wait()

    @pl.when(s >= 1)
    def _():
        @pl.loop(0, D // 128, unroll=7)
        def _(c):
            part = w_v[:, pl.ds(pl.multiple_of(c * 128, 128), 128)].astype(F32)
            gap = jnp.zeros((R - ROWS, 128), F32)
            wt[pl.ds(pl.multiple_of(c * 128, 128), 128), :] = jnp.concatenate([part, gap, part, gap], axis=0).T

        wt[pl.ds(D, 16), :] = jnp.zeros((16, 128), F32)

        @pl.when(s < 3)
        def _():
            @pl.loop(0, 64, unroll=8)
            def _(c):
                one = wt[pl.ds(pl.multiple_of(c * ROWS, 8), 32), :]
                two = wt[pl.ds(pl.multiple_of(c * ROWS + 32, 8), 32), :]
                le[pl.ds(pl.multiple_of(c * 32, 32), 32), pl.ds(0, 128)] = jnp.where(low, one, two).astype(BF16)

        @pl.when(s == 3)
        def _():
            @pl.loop(0, 7)
            def _(i):
                for j in range(8):
                    at = 512 * i + 256 * (j // 4) + 32 * (j % 4)
                    one = wt[pl.ds(pl.multiple_of(at, 32), 32), :]
                    two = wt[pl.ds(pl.multiple_of(at + 128, 32), 32), :]
                    l3[j, pl.ds(pl.multiple_of(i * 32, 32), 32), :] = jnp.where(low, one, two).astype(BF16)

            l3[:, pl.ds(224, 32), :] = jnp.zeros((8, 32, 128), BF16)

    pl.semaphore_wait(bar, 17)

    @pl.when(s < 3)
    def _():
        remote(s0_s, s0_r, s0_ss, s0_rs, s + 1, z, p).start()

    for dz in OFFSETS[:-1]:
        pl.semaphore_signal(line, inc=1, device_id=(s, lax.rem(z + dz, 8) * 8 + p), device_id_type=MESH)

    def turned_parts(packed):
        turned = pltpu.roll(packed, 64, 1)
        zero = jnp.zeros((32, 128), F32)
        return [
            part.astype(BF16) for part in (
                jnp.where(low, packed, zero), jnp.where(low, turned, zero),
                jnp.where(low, zero, turned), jnp.where(low, zero, packed),
            )
        ]

    def place(packed):
        for i, part in enumerate(turned_parts(packed)):
            rr[pl.ds(32 * i, 32), :] = part
            rr[pl.ds(128 + 32 * i, 32), :] = part

    def summed(slot, count=8):
        wait_bytes(zb.at[slot, pl.ds(0, count)], z_rs.at[slot])
        total = zb[slot, 0].astype(F32)
        for i in range(1, 8):
            total = total + zb[slot, i].astype(F32)
        return total

    def spread():
        for part, (lo, hi) in enumerate(PARTS):
            for i in range(lo, hi):
                at = pl.ds(pl.multiple_of(lax.rem(z + OFFSETS[i], 8) * 256, 256), 256)
                ob[:, i] = jnp.dot(le[at, :], rr[...], preferred_element_type=F32).astype(BF16).reshape(8, 32, 128)
            for j, (a, b) in enumerate(PLANE):
                to_p = plane(a, b)
                span = pl.ds(lo, hi - lo)
                remote(ob.at[to_p, span], pb.at[j, span], p_ss, p_rs.at[part], s, z, to_p).start()

    def relay():
        for part, (lo, hi) in enumerate(PARTS):
            wait_bytes(pb.at[pl.ds(0, hi - lo), pl.ds(0, 7)], p_rs.at[part])
            for i in range(lo, hi):
                total = ob[p, i].astype(F32)
                for j in range(7):
                    total = total + pb[j, i].astype(F32)
                zs[0, i] = total.astype(BF16)
                to_z = lax.rem(z + OFFSETS[i], 8)
                remote(zs.at[0, i], zb.at[0, z], z_ss.at[0], z_rs.at[0], s + 1, to_z, p).start()

    def send_columns():
        for dz in OFFSETS[:-1]:
            to_z = lax.rem(z + dz, 8)
            block = le.at[pl.ds(pl.multiple_of(to_z * 256, 256), 256), pl.ds(0, 128)]
            remote(block, lb.at[z], wa_ss, wa_rs, s, to_z, p).start()
        lb[z] = le[pl.ds(pl.multiple_of(z * 256, 256), 256), pl.ds(0, 128)]

    def line_product():
        wait_bytes(l3.at[pl.ds(0, 7)], wa_rs)
        total = jnp.zeros((TOK, 128), F32)
        for dz in nearest:
            from_z = lax.rem(z + dz, 8)
            if dz:
                wait_bytes(yz.at[from_z], v_rs.at[from_z])
            right = jnp.concatenate(turned_parts(yz[from_z].astype(F32)), axis=0)
            total = total + jnp.dot(lb[from_z], right, preferred_element_type=F32)
        bs[...] = total.reshape(8, 32, 128)
        bs[p] += yz[z].astype(F32)
        ar_s[...] = bs[...].reshape(TOK, 128).astype(BF16)
        for a, b in PLANE + ((0, 0),):
            remote(ar_s, ar_r.at[p], ar_ss, ar_rs, 3, z, plane(a, b)).start()

    def plane_product(k):
        total = jnp.zeros((TOK, 128), F32)
        for j in range(8):
            parts = turned_parts(yb[k, j].astype(F32))
            total = total + jnp.dot(lc[j], jnp.concatenate(parts + parts, axis=0), preferred_element_type=F32)
        zs[k] = total.astype(BF16).reshape(8, 32, 128)
        for dz in OFFSETS:
            to_z = lax.rem(z + dz, 8)
            if k == 2 and dz == 0:
                zb[1, z] = zs[k, z]
            else:
                remote(zs.at[k, to_z], zb.at[1, z], z_ss.at[k], z_rs.at[1], (0, 1, 3)[k], to_z, p).start()

    def share_plane(k):
        for a, b in PLANE:
            remote(yb.at[k, p], yb.at[k, p], y_ss.at[k], y_rs.at[k], s, z, plane(a, b)).start()

    def projected(tokens, both_proj):
        acc[...] = jnp.zeros((TOK, 128), F32)

        @pl.loop(0, 7)
        def _(c):
            at = pl.ds(pl.multiple_of(c * 512, 512), 512)
            acc[...] += nt(tokens[:, at], both_proj[:, at])

    def pass_queries(held, ss, rs, first=0, count=8):
        for a, b in PLANE:
            to_p = plane(a, b)

            @pl.loop(first, first + count)
            def _(i):
                block = held.at[i * 8 + p]
                remote(block, block, ss, rs, s, z, to_p).start()

    def turn_queries(held, turned, first=0, count=8):
        @pl.loop(8 * first, 8 * (first + count))
        def _(c):
            qf[pl.ds(pl.multiple_of(c * 64, 64), 64), :] = held[c].astype(F32)

        for t in range(32):
            rows = qf[pl.ds(512 * first + t, 16 * count, stride=32), :]
            turned[128 * t:128 * t + 128, 16 * first:16 * (first + count)] = rows.T.astype(BF16)

    def scored(turned):
        return jnp.dot(flat[...].astype(BF16), turned[...], preferred_element_type=F32)[0:8]

    def wait_queries(held, rs, blocks=56):
        wait_bytes(held.at[pl.ds(0, blocks)], rs)

    def go_ahead(to_s):
        pl.semaphore_signal(gate, inc=1, device_id=(to_s, d), device_id_type=MESH)

    def project_inputs():
        for c in loads[3:6]:
            c.wait()
        projected(act_v, pin_v)
        x2[...] = acc[...].astype(BF16)

    position = lax.broadcasted_iota(jnp.int32, (SEQ, 128), 0)

    def sketch(n, held):
        length = len_ref[n]
        rows = pl.ds(n * SEQ, SEQ)
        g = jnp.where(position < length, acc[rows, :], 0.0).astype(BF16)
        skf[...] = lax.dot_general(g, held[rows, :], (((0,), (0,)), ((), ())), preferred_element_type=F32)
        pairs = jnp.where(low, skf[pl.ds(0, 32, stride=2), :], skf[pl.ds(1, 32, stride=2), :])
        return pairs / jnp.full((32, 128), length, jnp.int32).astype(F32)

    def lay_flat(n, pairs, to):
        for t in range(32):
            to[pl.ds(n, 1), 128 * t:128 * t + 128] = pairs[t:t + 1, :]

    slot = jnp.minimum(s, 2)
    nearest = (0, 1, 7, 2, 6, 3, 5, 4)

    def gather_line(count=8):
        total = summed(1, count).astype(BF16)

        @pl.when(z < 7)
        def _():
            ag[d] = total
            for dz in OFFSETS[:-1]:
                remote(ag.at[d], ag.at[d], az_ss, az_rs.at[z], s, lax.rem(z + dz, 8), p).start()

    def gather_plane(distances):
        for dz in distances:
            from_z = lax.rem(z + dz, 8)

            @pl.when(from_z < 7)
            def _():
                block = ag.at[from_z * 8 + p]
                if dz:
                    wait_bytes(block, az_rs.at[from_z])
                for a, b in PLANE:
                    remote(block, block, ap_ss, ap_rs.at[from_z], s, z, plane(a, b)).start()

    def project_tokens():
        wide = lax.broadcasted_iota(jnp.int32, (128, 128), 1) < 64
        acc[...] = jnp.zeros((TOK, 128), F32)
        for group in ((0, 1, 7), (2, 6), (3, 5), (4,)):
            for dz in group:
                from_z = lax.rem(z + dz, 8)

                @pl.when(from_z < 7)
                def _():
                    wait_bytes(ag.at[pl.ds(0, 7)], ap_rs.at[from_z])

            total = acc[...]
            for dz in group:
                from_z = lax.rem(z + dz, 8)
                parts = []
                for c in range(2):
                    piece = ag[pl.ds(from_z * 8 + 4 * c, 4)].reshape(128, 128)
                    zero = jnp.zeros_like(piece)
                    parts += [jnp.where(wide, piece, zero), jnp.where(wide, zero, piece)]
                at = pl.ds(pl.multiple_of(lax.rem(from_z, 7) * 512, 512), 512)
                total = total + jnp.dot(top_v[:, at], jnp.concatenate(parts, axis=0), preferred_element_type=F32)
            acc[...] = total
        acc[...] = acc[...] + pltpu.roll(acc[...], 64, 1)

    @pl.when(s == 2)
    def _():
        send_columns()

    @pl.when((s == 1) | (s == 2))
    def _():
        wait_bytes(s0_r, s0_rs)
        place(s0_r[...].astype(F32))
        spread()

        @pl.when(s == 1)
        def _():
            go_ahead(0)

    @pl.when(s == 3)
    def _():
        for a, b in PLANE:
            to_p = plane(a, b)
            remote(l3.at[to_p], lc.at[p, :, pl.ds(0, 128)], wa_ss, wa_rs, s, z, to_p).start()
        lc[p, :, 0:128] = l3[p]
        wait_bytes(s0_r, s0_rs)
        yb[0, p] = s0_r[...]
        share_plane(0)

        @pl.loop(0, 8)
        def _(j):
            for i in range(8):
                at = 512 * i + lax.div(p, 4) * 256 + lax.rem(p, 4) * 32 + sub + 128 * half
                hit = (at - ROWS * (8 * z + j) == lane_i) & (lane_i < ROWS)
                lc[j, 32 * i:32 * i + 32, 128:256] = jnp.where(hit, 1.0, 0.0).astype(BF16)

    loads[2].wait()
    q32 = qry_v[...].astype(F32)
    for t in range(32):
        qf[pl.ds(t, 1), :] = q32[0:1, 128 * t:128 * t + 128]
        qf[pl.ds(32 + t, 1), :] = q32[1:2, 128 * t:128 * t + 128]
    qown[...] = qf[pl.ds(0, 64), :].astype(BF16)

    @pl.when(s == 1)
    def _():
        qb[d] = qown[...]


    @pl.when(s == 1)
    def _():
        for dz in OFFSETS[:-1]:
            remote(qown, qb.at[d], qz_ss, qz_rs, s, lax.rem(z + dz, 8), p).start()

    pl.semaphore_wait(line, 7)

    for at_s, to_s in ((0, 3), (2, 0)):
        @pl.when(s == at_s)
        def _():
            for dz in OFFSETS:
                remote(qown, qb.at[d], qz_ss, qz_rs, to_s, lax.rem(z + dz, 8), p).start()

    @pl.when(s == 3)
    def _():
        remote(qown, q3.at[d], qz_ss, q3z_rs, 1, z, p).start()

    @pl.when((s == 1) | (s == 2))
    def _():
        relay()

    @pl.when(s == 2)
    def _():
        yz[z] = summed(0).astype(BF16)
        for dz in OFFSETS[:-1]:
            remote(yz.at[z], yz.at[z], v_ss, v_rs.at[z], s, lax.rem(z + dz, 8), p).start()
        line_product()
        project_inputs()
        remote(x2, xr, x_ss, x_rs, 0, z, p).start()
        for c in loads[6:9]:
            c.wait()

    @pl.when(s == 3)
    def _():
        wait_bytes(l3.at[pl.ds(0, 7)], wa_rs)
        wait_bytes(yb.at[0, pl.ds(0, 7)], y_rs.at[0])
        plane_product(0)
        project_inputs()
        for c in loads[6:9]:
            c.wait()
        projected(top_v, pout_v)
        for n in range(2):
            sk_s[pl.ds(32 * n, 32), :] = sketch(n, x2).astype(BF16)
        remote(sk_s, sk_r, sk_ss, sk_rs, 1, z, p).start()
        wait_bytes(qb.at[pl.ds(0, 8)], qz_rs)
        pass_queries(qb, qp_ss.at[0], qp_rs.at[0], 0, 4)
        yb[1, p] = summed(0).astype(BF16)
        share_plane(1)
        wait_bytes(yb.at[1, pl.ds(0, 7)], y_rs.at[1])
        plane_product(1)
        wait_queries(qb, qp_rs.at[0], 28)
        turn_queries(qb, qg, 0, 4)
        wait_bytes(ar_r, ar_rs)
        total = ar_r[0].astype(F32)
        for i in range(1, 8):
            total = total + ar_r[i].astype(F32)
        yb[2] = total.reshape(8, 32, 128).astype(BF16)
        plane_product(2)
        pass_queries(qb, qp_ss.at[1], qp_rs.at[1], 4, 4)
        gather_line(7)

    def pass_own(blocks):
        wait_bytes(qb.at[pl.ds(0, blocks)], qz_rs)
        for i in range(2):
            pass_queries(qb, qp_ss.at[i], qp_rs.at[i], 4 * i, 4)

    @pl.when(s == 0)
    def _():
        pl.semaphore_wait(gate, 1)

    @pl.when(s == 1)
    def _():
        wait_bytes(q3.at[0], q3z_rs)
        for a, b in PLANE:
            remote(q3.at[d], q3.at[d], q3p_ss, q3p_rs, s, z, plane(a, b)).start()
        pass_own(7)

    @pl.when(s < 2)
    def _():
        project_inputs()
        for c in loads[6:9]:
            c.wait()

    @pl.when(s == 1)
    def _():
        wait_bytes(q3.at[pl.ds(0, 7)], q3p_rs)
        span = q3.at[pl.ds(pl.multiple_of(8 * z, 8), 8)]
        for dz in OFFSETS[:-1]:
            remote(span, span, q3v_ss, q3v_rs, s, lax.rem(z + dz, 8), p).start()

    @pl.when(s == 0)
    def _():
        remote(x2, xr, x_ss, x_rs, 3, z, p).start()

    def turn_own():
        for i in range(2):
            wait_queries(qb, qp_rs.at[i], 28)
            turn_queries(qb, qg, 4 * i, 4)

    @pl.when(s == 1)
    def _():
        turn_own()

    @pl.when(s < 2)
    def _():
        gather_line()

    @pl.when(s == 0)
    def _():
        pass_own(8)

    @pl.when(s != 2)
    def _():
        gather_plane(nearest[:1])

        @pl.when(s == 3)
        def _():
            wait_queries(qb, qp_rs.at[1], 28)
            turn_queries(qb, qg, 4, 4)

        gather_plane(nearest[1:])

        @pl.when(s == 1)
        def _():
            wait_queries(q3, q3v_rs)
            turn_queries(q3, qg3)
            xr[...] = x2[...]

        @pl.when(s != 1)
        def _():
            wait_bytes(xr, x_rs)

        project_tokens()
        flat[...] = jnp.zeros((16, R * R), F32)
        for n in range(2):
            lay_flat(n, sketch(n, xr), flat)

        @pl.when(s == 0)
        def _():
            turn_own()

        ex[slot] = scored(qg)

        @pl.when(s == 1)
        def _():
            wait_bytes(sk_r, sk_rs)
            for n in range(2):
                lay_flat(n, sk_r[pl.ds(32 * n, 32), :].astype(F32), flat)
            ex[slot] += scored(qg3)

        for j in (2, 3, 1):
            remote(ex.at[slot], ex.at[slot], ex_ss, ex_rs, lax.rem(s + j, 4), z, p).start()

    @pl.when(s < 3)
    def _():
        wait_bytes(s0_s, s0_ss)

    @pl.when(s != 2)
    def _():
        wait_bytes(ag.at[pl.ds(0, 49)], ap_ss)
        for i in range(2):
            wait_bytes(qb.at[pl.ds(0, 28)], qp_ss.at[i])

        @pl.when(z < 7)
        def _():
            wait_bytes(ag.at[pl.ds(0, 7)], az_ss)

    @pl.when(s == 1)
    def _():
        wait_bytes(qb.at[pl.ds(0, 7)], qz_ss)
        wait_bytes(q3.at[pl.ds(0, 7)], q3p_ss)
        wait_bytes(q3.at[pl.ds(0, 56)], q3v_ss)

    @pl.when(s == 3)
    def _():
        wait_bytes(qown, qz_ss)

    @pl.when((s == 0) | (s == 2))
    def _():
        wait_bytes(qb.at[pl.ds(0, 8)], qz_ss)

    @pl.when((s == 0) | (s == 2))
    def _():
        wait_bytes(xr, x_ss)

    @pl.when(s == 3)
    def _():
        wait_bytes(sk_s, sk_ss)

    @pl.when((s == 1) | (s == 2))
    def _():
        wait_bytes(pb, p_ss)
        wait_bytes(zs.at[0], z_ss.at[0])

    @pl.when(s >= 2)
    def _():
        wait_bytes(l3.at[pl.ds(0, 7)], wa_ss)

    @pl.when(s == 2)
    def _():
        wait_bytes(yz.at[pl.ds(0, 7)], v_ss)
        wait_bytes(ar_r, ar_ss)

    @pl.when(s == 3)
    def _():
        for k in range(2):
            wait_bytes(zs.at[k], z_ss.at[k])
        wait_bytes(zs.at[2, pl.ds(0, 7)], z_ss.at[2])
        for k in range(2):
            wait_bytes(yb.at[k, pl.ds(0, 7)], y_ss.at[k])

    @pl.when(s != 2)
    def _():
        wait_bytes(ex.at[pl.ds(0, 2)], ex_rs)

    @pl.when(s == 2)
    def _():
        wait_bytes(ex, ex_rs)
    total = ex[0] + ex[1] + ex[2]
    mine = jnp.zeros((8, 32), F32)
    for i in range(4):
        mine = mine + jnp.where(s == i, total[:, 32 * i:32 * i + 32], 0.0)
    out_ref[...] = mine[0:2, :]

    @pl.when(s != 2)
    def _():
        wait_bytes(ex, ex_ss)


def local(top_grad, activations, weights, proj_in, proj_out, queries, lengths):
    dma = pltpu.SemaphoreType.DMA
    anywhere = pl.BlockSpec(memory_space=pl.ANY)
    return pl.pallas_call(
        kernel,
        out_shape=jax.ShapeDtypeStruct((2, 32), F32),
        in_specs=[anywhere] * 6 + [pl.BlockSpec(memory_space=pltpu.SMEM)],
        out_specs=pl.BlockSpec(memory_space=pltpu.VMEM),
        scratch_shapes=[
            pltpu.VMEM((ROWS, D), BF16),
            pltpu.VMEM((R, 256), BF16),
            pltpu.VMEM((2, R * R), BF16),
            pltpu.VMEM((2 * R, D), BF16),
            pltpu.VMEM((2 * R, D), BF16),
            pltpu.VMEM((TOK, D), BF16),
            pltpu.VMEM((TOK, D), BF16),
            pltpu.VMEM((D + 16, 128), F32),
            pltpu.VMEM((2048, 256), BF16),
            pltpu.VMEM((8, 256, 128), BF16),
            pltpu.VMEM((8, 256, 128), BF16),
            pltpu.VMEM((8, 256, 256), BF16),
            pltpu.VMEM((256, 128), BF16),
            pltpu.VMEM((32, 128), BF16),
            pltpu.VMEM((32, 128), BF16),
            pltpu.VMEM((8, 8, 32, 128), BF16),
            pltpu.VMEM((7, 8, 32, 128), BF16),
            pltpu.VMEM((8, 32, 128), BF16),
            pltpu.VMEM((3, 8, 32, 128), BF16),
            pltpu.VMEM((8, 32, 128), F32),
            pltpu.VMEM((TOK, 128), BF16),
            pltpu.VMEM((8, TOK, 128), BF16),
            pltpu.VMEM((3, 8, 32, 128), BF16),
            pltpu.VMEM((2, 8, 32, 128), BF16),
            pltpu.VMEM((64, 32, 128), BF16),
            pltpu.VMEM((64, 128), BF16),
            pltpu.VMEM((64, 64, 128), BF16),
            pltpu.VMEM((64, 64, 128), BF16),
            pltpu.VMEM((4096, 128), F32),
            pltpu.VMEM((R * R, 128), BF16),
            pltpu.VMEM((R * R, 128), BF16),
            pltpu.VMEM((TOK, 128), F32),
            pltpu.VMEM((TOK, 128), BF16),
            pltpu.VMEM((TOK, 128), BF16),
            pltpu.VMEM((128, 128), F32),
            pltpu.VMEM((64, 128), BF16),
            pltpu.VMEM((64, 128), BF16),
            pltpu.VMEM((16, R * R), F32),
            pltpu.VMEM((3, 8, 128), F32),
            dma((9,)),
            dma, dma,
            dma, dma((4,)),
            dma((3,)), dma((2,)),
            dma, dma((8,)),
            dma, dma((8,)),
            dma, dma, dma((2,)), dma((2,)),
            dma, dma, dma, dma((8,)), dma((2,)), dma((2,)), dma, dma,
            dma, dma, dma, dma, dma, dma, dma, dma, dma,
            dma, dma,
            pltpu.SemaphoreType.REGULAR,
            pltpu.SemaphoreType.REGULAR,
        ],
        compiler_params=pltpu.CompilerParams(
            collective_id=0, has_side_effects=True, vmem_limit_bytes=56541184
        ),
        name="chain",
    )(top_grad, activations, weights, proj_in, proj_out, queries, lengths) * 0.125


def solution(mesh):
    in_specs = (
        P("dp", None),
        P("section", "dp", None),
        P("section", "dp", None),
        P("section", None, None),
        P("section", None, None),
        P("section", "dp", None),
        P("dp"),
    )
    return jax.shard_map(local, mesh=mesh, in_specs=in_specs, out_specs=P("dp", "section"), check_vma=False)
```
